128 devices in a mesh: seq: 32 (over z, y_lo, x), tp: 4 (over y_hi, core).
Axes of the slice: x: 4, y: 4 (y_hi: 2, y_lo: 2; y = y_hi * 2 + y_lo), z: 4, core: 2. Of those that a mesh axis runs over, the one named last changes fastest.
Arguments:
- hidden: bfloat16 [8192, 3072], P('seq'), may hold values from -6 to 6
- qkv_weight: bfloat16 [3072, 3, 1536], P(None, None, 'tp'), may hold values from -0.109375 to 0.109375
- cotangent: bfloat16 [8192, 1536], P('seq', 'tp'), may hold values from -6 to 6
Outputs:
- attention: bfloat16 [8192, 1536], P('seq', 'tp')
- grad_hidden: bfloat16 [8192, 3072], P('seq', 'tp')
- grad_weight: float32 [3072, 3, 1536], P('seq', None, 'tp')
The draws below stay inside these ranges and needn't reach their ends.
All inputs are finite; a program needn't handle non-finite values.
Results may differ from the reference program's by a relative error of at most 0.023.
Values may be sent and summed in bfloat16 or wider, within the bound.
A program may use at most 128 MiB of HBM per device.

```python
import math
import jax
import jax.numpy as jnp
from jax import lax

D = 3072
HEADS = 12
HD = 128
TOK_DEV = 256
TOKENS = 8192
N_SEQ = 32


def draw_hidden(key, part):
    key = jax.random.fold_in(key, 11)
    base_key = jax.random.fold_in(key, 0)
    values = jnp.clip(jax.random.normal(base_key, (TOKENS, D), jnp.float32), -6.0, 6.0)
    return values.astype(jnp.bfloat16)


def levels(stream_key, shape, cuts, least, high):
    loudness, own = 1.0, jax.random.fold_in(stream_key, 6)
    for axis_at, blocks in cuts:
        draws = jnp.exp(jax.random.uniform(jax.random.fold_in(own, axis_at), (blocks,), jnp.float32, least / len(cuts), high / len(cuts)))
        loudness = loudness * jnp.repeat(draws, shape[axis_at] // blocks).reshape([-1 if axis == axis_at else 1 for axis in range(len(shape))])
    return loudness


def bell_draw(rng, shape, width, most, pieces=(), held_as=jnp.bfloat16):
    entries = jax.random.normal(rng, shape, jnp.float32) * width
    if len(pieces) > 0:
        entries = levels(rng, shape, pieces, -0.22, 0.18) * entries
    return jnp.clip(entries, min=-most, max=most).astype(held_as)


def setup_inputs(seed: int = 0) -> dict:
    key_list = jax.random.split(jax.random.key(seed), 4)
    hidden = draw_hidden(jax.random.fold_in(key_list[3], 71), 0)
    qkv_weight = bell_draw(key_list[1], (D, 3, HEADS * HD), D ** -0.5, 0.109375, ((2, 4),))
    cotangent = bell_draw(key_list[2], (TOKENS, HEADS * HD), 1.0, 6.0, ((0, 32), (1, 4)))
    return dict(hidden=hidden, qkv_weight=qkv_weight, cotangent=cotangent)


def head_pass(operands):
    query, key_rows, value_rows, grad_out = operands
    softmax_scale = 1.0 / math.sqrt(HD)

    def block_step(carry, block):
        key_acc, value_acc = carry
        query_block, grad_block = block
        scores = jnp.dot(query_block, key_rows.T, preferred_element_type=jnp.float32) * softmax_scale
        top_score = lax.optimization_barrier(jnp.max(scores, axis=-1, keepdims=True))
        log_total = top_score + jnp.log(lax.optimization_barrier(jnp.sum(jnp.exp(scores - top_score), axis=-1, keepdims=True)))
        weights = jnp.exp(scores - log_total).astype(jnp.bfloat16)
        output = jnp.dot(weights, value_rows, preferred_element_type=jnp.float32).astype(jnp.bfloat16)
        grad_probs = jnp.dot(grad_block, value_rows.T, preferred_element_type=jnp.float32)
        row_delta = lax.optimization_barrier(jnp.sum(grad_block.astype(jnp.float32) * output.astype(jnp.float32), axis=-1, keepdims=True))
        grad_scores = (weights.astype(jnp.float32) * (grad_probs - row_delta)).astype(jnp.bfloat16)
        grad_query = (jnp.dot(grad_scores, key_rows, preferred_element_type=jnp.float32) * softmax_scale).astype(jnp.bfloat16)
        key_acc = key_acc + jnp.dot(grad_scores.T, query_block, preferred_element_type=jnp.float32)
        value_acc = value_acc + jnp.dot(weights.T, grad_block, preferred_element_type=jnp.float32)
        return ((key_acc, value_acc), (output, grad_query))
    zeros = jnp.zeros((TOKENS, HD), jnp.float32)
    blocks = (query.reshape(N_SEQ, TOK_DEV, HD), grad_out.reshape(N_SEQ, TOK_DEV, HD))
    (key_acc, value_acc), (outputs, grad_queries) = lax.scan(block_step, (zeros, zeros), blocks)
    grad_key = (key_acc * softmax_scale).astype(jnp.bfloat16)
    grad_value = value_acc.astype(jnp.bfloat16)
    return (outputs.reshape(TOKENS, HD), grad_queries.reshape(TOKENS, HD), grad_key, grad_value)

def reference(hidden, qkv_weight, cotangent):
    hidden_wide = hidden.astype(jnp.float32)
    weight_wide = qkv_weight.astype(jnp.float32)
    projected = jnp.einsum('td,dcj->tcj', hidden_wide, weight_wide).astype(jnp.bfloat16)
    split = projected.reshape(TOKENS, 3, HEADS, HD).transpose(1, 2, 0, 3)
    grad_heads = cotangent.reshape(TOKENS, HEADS, HD).transpose(1, 0, 2)
    outputs, grad_query, grad_key, grad_value = lax.map(head_pass, (split[0], split[1], split[2], grad_heads))
    attention = outputs.transpose(1, 0, 2).reshape(TOKENS, HEADS * HD)
    grad_proj = jnp.stack([grad_query, grad_key, grad_value], axis=0).transpose(2, 0, 1, 3).reshape(TOKENS, 3, HEADS * HD)
    grad_wide = grad_proj.astype(jnp.float32)
    grad_weight = jnp.einsum('td,tcj->dcj', hidden_wide, grad_wide)
    grad_hidden = jnp.einsum('tcj,dcj->td', grad_wide, weight_wide).astype(jnp.bfloat16)
    return (attention, grad_hidden, grad_weight)
```

```python
import functools
import math

import jax
import jax.numpy as jnp
from jax import lax
from jax.experimental import pallas as pl
from jax.experimental.pallas import tpu as pltpu
from jax.sharding import PartitionSpec as P

HD = 128
T = 256
NZ, NY, NX = 4, 2, 4
KEYS = NZ * NY * T
CHUNK = 512
SCALE = 1.0 / math.sqrt(HD)
LOG2 = SCALE * math.log2(math.e)
MESH = pl.DeviceIdType.MESH
F32, BF16 = jnp.float32, jnp.bfloat16
NN = (((1,), (0,)), ((), ()))
NT = (((1,), (1,)), ((), ()))


def dot(a, b, dims=NN):
    return lax.dot_general(a, b, dims, preferred_element_type=F32)


def coords():
    s = lax.axis_index("seq")
    return s // (NY * NX), (s // NX) % NY, s % NX, lax.axis_index("tp")


def seq_of(z, y, x):
    return (z * NY + y) * NX + x


def aligned(i, n):
    return pl.ds(pl.multiple_of(i * n, n), n)


def attention_kernel(
    p_ref, cot_ref, ht_ref, att_ref, g_ref, hx_ref,
    own_qg, own_kv, qg, kv, vkt, pt, ut, s_buf, st, sm, sm_all, ma, cs, es, rhs, ob, ro, kb, rk,
    sem_s, sem_r, sem_os, sem_or, sem_ks, sem_kr, sem_l,
):
    z, y, x, t = coords()
    other = 1 - y
    head_a, head_b = 2 * y, 2 - 2 * y

    def at(zz, yy, xx):
        return (seq_of(zz, yy, xx), t)

    def xs(d):
        return (x + d) % NX

    def zs(d):
        return (z + d) % NZ

    for h in range(3):
        cols = slice(h * HD, (h + 1) * HD)
        own_qg[h, 0] = p_ref[0, :, cols]
        own_qg[h, 1] = cot_ref[:, cols]
        own_kv[h, 0] = p_ref[1, :, cols]
        own_kv[h, 1] = p_ref[2, :, cols]

    barrier = pltpu.get_barrier_semaphore()
    peers = [at(z, y, xs(d)) for d in (1, 2, 3)] + [at(z, other, xs(d)) for d in range(4)]
    peers += [at(zs(d), y, x) for d in (1, 2, 3)] + [at(zs(d), other, x) for d in (1, 2, 3)]
    for peer in peers:
        pl.semaphore_signal(barrier, inc=1, device_id=peer, device_id_type=MESH)
    pl.semaphore_wait(barrier, len(peers))

    def remote(i, src, dst, peer):
        return pltpu.make_async_remote_copy(
            src_ref=src, dst_ref=dst, send_sem=sem_s.at[i], recv_sem=sem_r.at[i],
            device_id=peer, device_id_type=MESH,
        )

    def qg_slot(yy, xx):
        return qg.at[4 + yy * NX + xx]

    def kv_rows(j, yy, zz):
        return kv.at[j, :, aligned(yy * NZ + zz, T), :]

    first = [
        remote(0, own_qg.at[head_b], qg_slot(y, x), at(z, other, x)),
        remote(1, own_kv.at[1], kv_rows(0, y, z), at(z, other, x)),
        remote(2, own_kv.at[head_b], kv_rows(1, y, z), at(z, other, x)),
    ]
    for d in (1, 2, 3):
        first.append(remote(2 + d, own_qg.at[1], qg.at[x], at(z, y, xs(d))))
        first.append(remote(8 + d, own_kv.at[1], kv_rows(0, y, z), at(zs(d), y, x)))
    for d in (1, 2, 3):
        first.append(remote(5 + d, own_qg.at[head_a], qg_slot(y, x), at(z, y, xs(d))))
        first.append(remote(11 + d, own_kv.at[head_a], kv_rows(1, y, z), at(zs(d), y, x)))
    for c in first:
        c.start()
    qg[x] = own_qg[1]
    qg[4 + y * NX + x] = own_qg[head_a]
    kv[0, :, aligned(y * NZ + z, T), :] = own_kv[1]
    kv[1, :, aligned(y * NZ + z, T), :] = own_kv[head_a]
    sm[...] = jnp.zeros_like(sm)
    ma[...] = jnp.zeros_like(ma)

    def got(i, dst):
        remote(i, dst, dst, at(z, other, x)).wait_recv()

    relay = []
    got(0, qg_slot(other, x))
    for d in (1, 2, 3):
        relay.append(remote(14 + d, qg_slot(other, x), qg_slot(other, x), at(z, y, xs(d))))
        relay[-1].start()
    for j in (0, 1):
        got(1 + j, kv_rows(j, other, z))
        for d in (1, 2, 3):
            rows = kv_rows(j, other, z)
            relay.append(remote(17 + 3 * j + d, rows, rows, at(zs(d), y, x)))
            relay[-1].start()
    hx_copies = [remote(26 + d, ht_ref.at[:, xs(d)], hx_ref.at[x], at(z, y, xs(d))) for d in (1, 2, 3)]
    for c in hx_copies:
        c.start()
    hx_own = pltpu.make_async_copy(ht_ref.at[:, x], hx_ref.at[x], sem_l.at[0])
    hx_own.start()

    for d in (1, 2, 3):
        got(2 + d, qg.at[xs(4 - d)])
        got(5 + d, qg_slot(y, xs(4 - d)))
        got(8 + d, kv_rows(0, y, zs(4 - d)))
        got(11 + d, kv_rows(1, y, zs(4 - d)))
        got(14 + d, qg_slot(other, xs(4 - d)))
        got(17 + d, kv_rows(0, other, zs(4 - d)))
        got(20 + d, kv_rows(1, other, zs(4 - d)))

    def transpose_block(i, _):
        for j in (0, 1):
            vkt[j, 0:HD, aligned(i, T)] = kv[j, 1, aligned(i, T), :].T
            vkt[j, HD : 2 * HD, aligned(i, T)] = kv[j, 0, aligned(i, T), :].T
        return 0

    lax.fori_loop(0, KEYS // T, transpose_block, 0)

    def unit(j, u):
        q, g = qg[u, 0], qg[u, 1]
        chunks = [slice(c * CHUNK, (c + 1) * CHUNK) for c in range(KEYS // CHUNK)]
        top = None
        for c in chunks:
            s = dot(kv[j, 0, c, :], q, NT)
            s_buf[c] = s
            m = jnp.max(s, axis=0, keepdims=True)
            top = m if top is None else jnp.maximum(top, m)
        top = top * LOG2
        total, out = 0.0, 0.0
        for c in chunks:
            p = jnp.exp2(s_buf[c] * LOG2 - top)
            total = total + jnp.sum(p, axis=0, keepdims=True)
            p = p.astype(BF16)
            pt[u, c, :] = p
            out = out + dot(vkt[j, :, c], p)
        g_t = g.astype(F32).T
        delta = jnp.sum(g_t * out[:HD], axis=0, keepdims=True) / total
        grad = 0.0
        for c in chunks:
            dp = dot(kv[j, 1, c, :], g, NT)
            d = (pt[u, c, :].astype(F32) * (dp - delta)).astype(BF16)
            ut[u, c, :] = d
            grad = grad + dot(vkt[j, HD:, c], d)
        st[u, : 2 * HD] = out
        st[u, 2 * HD :] = grad
        sm[0, pl.ds(u, 1), :] = top + jnp.log2(total)
        sm[1, pl.ds(u, 1), :] = delta
        ma[pl.ds(u, 1), :] = top
        return 0

    lax.fori_loop(0, 4, lambda u, _: unit(0, u), 0)
    lax.fori_loop(4, 12, lambda u, _: unit(1, u), 0)

    stats = [remote(23 + d, sm, sm_all.at[x], at(z, y, xs(d))) for d in (1, 2, 3)]
    for c in stats:
        c.start()
    sm_all[x] = sm[...]
    for d in (1, 2, 3):
        got(23 + d, sm_all.at[xs(4 - d)])
    lse = sm_all[:, 0]
    top = jnp.max(lse, axis=0)
    lse_all = top + jnp.log2(jnp.sum(jnp.exp2(lse - top), axis=0))
    delta = jnp.sum(jnp.exp2(lse - lse_all) * sm_all[:, 1], axis=0)
    cs[...] = jnp.exp2(ma[...] - lse_all)
    es[...] = delta - sm[1]

    def prepare(u):
        c, e = cs[pl.ds(u, 1), :], es[pl.ds(u, 1), :]
        o = st[u, 0:HD] * c
        dq = (st[u, 2 * HD :] - e * st[u, HD : 2 * HD]) * (c * SCALE)
        ob[u, 0] = o.T.astype(BF16)
        ob[u, 1] = dq.T.astype(BF16)
        cols = jnp.concatenate([c, e, jnp.zeros((6, T), F32)], axis=0).T
        c, e = cols[:, 0:1], cols[:, 1:2]
        cq = c * qg[u, 0].astype(F32)
        rhs[u, :, 0:HD] = (c * qg[u, 1].astype(F32)).astype(BF16)
        rhs[u, :, HD : 2 * HD] = (e * cq).astype(BF16)
        rhs[u, :, 2 * HD :] = cq.astype(BF16)

    def send_o(kind, d):
        xx = xs(d)
        u, h, yy = ((xx, 1, y), (4 + y * NX + xx, head_a, y), (4 + other * NX + xx, head_a, other))[kind]
        return u, pltpu.make_async_remote_copy(
            src_ref=ob.at[u], dst_ref=ro.at[h, x], send_sem=sem_os.at[kind, d], recv_sem=sem_or.at[kind, d],
            device_id=at(z, yy, xx), device_id_type=MESH,
        )

    def each_o(do):
        lax.fori_loop(1, 4, lambda d, _: do(0, d), 0)
        lax.fori_loop(0, 4, lambda d, _: do(2, d), 0)
        lax.fori_loop(1, 4, lambda d, _: do(1, d), 0)

    def prepare_send(kind, d):
        u, copy = send_o(kind, d)
        prepare(u)
        copy.start()
        return 0

    each_o(prepare_send)
    prepare(x)
    ro[1, x] = ob[x]
    prepare(4 + y * NX + x)
    ro[head_a, x] = ob[4 + y * NX + x]

    def send_k(j, own, d):
        yy = y if own else other
        zz = zs(d)
        b = j * 8 + yy * NZ + zz
        kind = 2 * j + (0 if own else 1)
        return yy * NZ + zz, b, pltpu.make_async_remote_copy(
            src_ref=kb.at[b], dst_ref=rk.at[j * 8 + y * NZ + z], send_sem=sem_ks.at[kind, d],
            recv_sem=sem_kr.at[kind, d], device_id=at(zz, yy, x), device_id_type=MESH,
        )

    def key_block(j, i, b):
        units = range(4) if j == 0 else range(4, 12)
        rows = aligned(i, T)
        dv = dk = 0.0
        for u in units:
            dv = dv + dot(pt[u, rows, :], rhs[u, :, : 2 * HD])
            dk = dk + dot(ut[u, rows, :], rhs[u, :, 2 * HD :])
        kb[b, 0] = ((dk - dv[:, HD:]) * SCALE).astype(BF16)
        kb[b, 1] = dv[:, :HD].astype(BF16)

    def key_send(j, own, d):
        i, b, copy = send_k(j, own, d)
        key_block(j, i, b)
        copy.start()
        return 0

    def each_k(do):
        for j in (0, 1):
            lax.fori_loop(0, 4, lambda d, _: do(j, False, d), 0)
            lax.fori_loop(1, 4, lambda d, _: do(j, True, d), 0)

    each_k(key_send)
    mine = y * NZ + z
    for j in (0, 1):
        key_block(j, mine, j * 8 + mine)
        rk[j * 8 + mine] = kb[j * 8 + mine]

    def finish_o(kind, d):
        _, copy = send_o(kind, d)
        copy.wait_send()
        xx = xs(4 - d)
        h = (1, head_a, head_b)[kind]
        pltpu.make_async_remote_copy(
            src_ref=ob.at[0], dst_ref=ro.at[h, xx], send_sem=sem_os.at[kind, d], recv_sem=sem_or.at[kind, d],
            device_id=at(z, other, x), device_id_type=MESH,
        ).wait_recv()
        return 0

    each_o(finish_o)
    for h in range(3):
        cols = slice(h * HD, (h + 1) * HD)
        for part in (0, 1):
            v = ro[h, 0, part].astype(F32)
            for xx in range(1, NX):
                v = v + ro[h, xx, part].astype(F32)
            if part == 0:
                att_ref[:, cols] = v.astype(BF16)
            else:
                g_ref[0, :, cols] = v.astype(BF16)

    def finish_k(j, own, d):
        _, _, copy = send_k(j, own, d)
        copy.wait_send()
        yy = y if own else other
        kind = 2 * j + (0 if own else 1)
        pltpu.make_async_remote_copy(
            src_ref=kb.at[0], dst_ref=rk.at[j * 8 + yy * NZ + zs(4 - d)], send_sem=sem_ks.at[kind, d],
            recv_sem=sem_kr.at[kind, d], device_id=at(z, other, x), device_id_type=MESH,
        ).wait_recv()
        return 0

    each_k(finish_k)
    for h, slots in ((1, range(8)), (0, range(8, 12)), (2, range(12, 16))):
        cols = slice(h * HD, (h + 1) * HD)
        for part in (0, 1):
            v = 0.0
            for i in slots:
                v = v + rk[i, part].astype(F32)
            g_ref[1 + part, :, cols] = v.astype(BF16)

    for c in first + relay + stats + hx_copies:
        c.wait_send()
    hx_own.wait()
    for d in (1, 2, 3):
        got(26 + d, hx_ref.at[xs(4 - d)])


def attention_call(projected, cotangent, hidden_t):
    scratch = [
        pltpu.VMEM((3, 2, T, HD), BF16),
        pltpu.VMEM((3, 2, T, HD), BF16),
        pltpu.VMEM((12, 2, T, HD), BF16),
        pltpu.VMEM((2, 2, KEYS, HD), BF16),
        pltpu.VMEM((2, 2 * HD, KEYS), BF16),
        pltpu.VMEM((12, KEYS, T), BF16),
        pltpu.VMEM((12, KEYS, T), BF16),
        pltpu.VMEM((KEYS, T), F32),
        pltpu.VMEM((12, 3 * HD, T), F32),
        pltpu.VMEM((2, 16, T), F32),
        pltpu.VMEM((NX, 2, 16, T), F32),
        pltpu.VMEM((16, T), F32),
        pltpu.VMEM((16, T), F32),
        pltpu.VMEM((16, T), F32),
        pltpu.VMEM((12, T, 3 * HD), BF16),
        pltpu.VMEM((12, 2, T, HD), BF16),
        pltpu.VMEM((3, NX, 2, T, HD), BF16),
        pltpu.VMEM((16, 2, T, HD), BF16),
        pltpu.VMEM((16, 2, T, HD), BF16),
        pltpu.SemaphoreType.DMA((30,)),
        pltpu.SemaphoreType.DMA((30,)),
        pltpu.SemaphoreType.DMA((3, 4)),
        pltpu.SemaphoreType.DMA((3, 4)),
        pltpu.SemaphoreType.DMA((4, 4)),
        pltpu.SemaphoreType.DMA((4, 4)),
        pltpu.SemaphoreType.DMA((1,)),
    ]
    vmem = pl.BlockSpec(memory_space=pltpu.VMEM)
    hbm = pl.BlockSpec(memory_space=pl.ANY)
    return pl.pallas_call(
        attention_kernel,
        out_shape=(
            jax.ShapeDtypeStruct((T, 3 * HD), BF16),
            jax.ShapeDtypeStruct((3, T, 3 * HD), BF16),
            jax.ShapeDtypeStruct((NX, NZ * NY, 96, T), BF16),
        ),
        in_specs=[vmem, vmem, hbm],
        out_specs=(vmem, vmem, hbm),
        scratch_shapes=scratch,
        compiler_params=pltpu.CompilerParams(
            collective_id=0, has_side_effects=True, vmem_limit_bytes=58 * 2**20
        ),
        cost_estimate=pl.CostEstimate(flops=12 * 10**9, bytes_accessed=4 * 10**6, transcendentals=6 * 10**6),
        name="attention_tile",
    )(projected, cotangent, hidden_t)


def weight_kernel(g_ref, hx_ref, w_ref, dw_ref, dh_ref, gx, dwb, dwr, dhb, dhr, sem_gs, sem_gr, sem_ws, sem_wr, sem_hs, sem_hr):
    z, y, x, t = coords()
    zy = z * NY + y
    me = lax.axis_index("seq")

    def xs(d):
        return (x + d) % NX

    def block(d):
        return (zy + d) % (NZ * NY)

    def ts(d):
        return (t + d) % 4

    barrier = pltpu.get_barrier_semaphore()
    peers = [(zy * NX + xs(d), t) for d in (1, 2, 3)] + [(block(d) * NX + x, t) for d in range(1, 8)]
    peers += [(me, ts(d)) for d in (1, 2, 3)]
    for peer in peers:
        pl.semaphore_signal(barrier, inc=1, device_id=peer, device_id_type=MESH)
    pl.semaphore_wait(barrier, len(peers))

    def send_g(c, d):
        return pltpu.make_async_remote_copy(
            src_ref=g_ref.at[c], dst_ref=gx.at[x, c], send_sem=sem_gs.at[c, d], recv_sem=sem_gr.at[c, d],
            device_id=(zy * NX + xs(d), t), device_id_type=MESH,
        )

    def send_w(c, d):
        return pltpu.make_async_remote_copy(
            src_ref=dwb.at[block(d), c], dst_ref=dwr.at[zy, c], send_sem=sem_ws.at[c, d], recv_sem=sem_wr.at[c, d],
            device_id=(block(d) * NX + x, t), device_id_type=MESH,
        )

    def send_h(d):
        return pltpu.make_async_remote_copy(
            src_ref=dhb.at[ts(d)], dst_ref=dhr.at[t], send_sem=sem_hs.at[d], recv_sem=sem_hr.at[d],
            device_id=(me, ts(d)), device_id_type=MESH,
        )

    for c in range(3):
        for d in (1, 2, 3):
            send_g(c, d).start()
    gx[x] = g_ref[...]

    def hidden_part(d):
        to = ts(d)
        for i in range(3):
            v = 0.0
            for c in range(3):
                rows = pl.ds(pl.multiple_of(to * 768 + i * 256, 256), 256)
                v = v + dot(g_ref[c], w_ref[c, rows, :], NT)
            dhb[to, :, i * 256 : (i + 1) * 256] = v.astype(BF16)

    def hidden_send(d, _):
        hidden_part(d)
        send_h(d).start()
        return 0

    lax.fori_loop(1, 4, hidden_send, 0)
    hidden_part(0)
    dhr[t] = dhb[t]

    for c in range(3):
        for d in (1, 2, 3):
            pltpu.make_async_remote_copy(
                src_ref=g_ref.at[c], dst_ref=gx.at[xs(4 - d), c], send_sem=sem_gs.at[c, d],
                recv_sem=sem_gr.at[c, d], device_id=(zy * NX + xs(d), t), device_id_type=MESH,
            ).wait_recv()

        def rows_of(i, _):
            v = 0.0
            for xx in range(NX):
                h = hx_ref[xx, pl.ds(i * 4, 4)].reshape(4 * 96, T)
                v = v + dot(h, gx[xx, c])
            dwb[pl.ds(i * 4, 4), c] = v.astype(BF16).reshape(4, 96, 384)
            return 0

        lax.fori_loop(0, 2, rows_of, 0)
        for d in range(1, 8):
            send_w(c, d).start()
        dwr[zy, c] = dwb[zy, c]

    for d in (1, 2, 3):
        pltpu.make_async_remote_copy(
            src_ref=dhb.at[0], dst_ref=dhr.at[ts(4 - d)], send_sem=sem_hs.at[d], recv_sem=sem_hr.at[d],
            device_id=(me, ts(d)), device_id_type=MESH,
        ).wait_recv()
    v = dhr[0].astype(F32)
    for i in range(1, 4):
        v = v + dhr[i].astype(F32)
    dh_ref[...] = v.astype(BF16)

    for c in range(3):
        for d in range(1, 8):
            pltpu.make_async_remote_copy(
                src_ref=dwb.at[0, c], dst_ref=dwr.at[block(8 - d), c], send_sem=sem_ws.at[c, d],
                recv_sem=sem_wr.at[c, d], device_id=(block(d) * NX + x, t), device_id_type=MESH,
            ).wait_recv()
        v = dwr[0, c].astype(F32)
        for i in range(1, 8):
            v = v + dwr[i, c].astype(F32)
        dw_ref[c] = v

    for c in range(3):
        for d in (1, 2, 3):
            send_g(c, d).wait_send()
        for d in range(1, 8):
            send_w(c, d).wait_send()
    for d in (1, 2, 3):
        send_h(d).wait_send()


def weight_call(grad_proj, hidden_x, weight):
    vmem = pl.BlockSpec(memory_space=pltpu.VMEM)
    return pl.pallas_call(
        weight_kernel,
        out_shape=(jax.ShapeDtypeStruct((3, 96, 384), F32), jax.ShapeDtypeStruct((T, 768), BF16)),
        in_specs=[vmem] * 3,
        out_specs=(vmem, vmem),
        scratch_shapes=[
            pltpu.VMEM((NX, 3, T, 384), BF16),
            pltpu.VMEM((8, 3, 96, 384), BF16),
            pltpu.VMEM((8, 3, 96, 384), BF16),
            pltpu.VMEM((4, T, 768), BF16),
            pltpu.VMEM((4, T, 768), BF16),
            pltpu.SemaphoreType.DMA((3, 4)),
            pltpu.SemaphoreType.DMA((3, 4)),
            pltpu.SemaphoreType.DMA((3, 8)),
            pltpu.SemaphoreType.DMA((3, 8)),
            pltpu.SemaphoreType.DMA((4,)),
            pltpu.SemaphoreType.DMA((4,)),
        ],
        compiler_params=pltpu.CompilerParams(
            collective_id=1, has_side_effects=True, vmem_limit_bytes=48 * 2**20
        ),
        cost_estimate=pl.CostEstimate(flops=4 * 10**9, bytes_accessed=10 * 10**6, transcendentals=0),
        name="weight_tail",
    )(grad_proj, hidden_x, weight)


def on_device(hidden, qkv_weight, cotangent):
    weight = qkv_weight.transpose(1, 0, 2)
    projected = jnp.einsum("td,cdj->ctj", hidden, weight, preferred_element_type=F32).astype(BF16)
    hidden_t = hidden.T.reshape(NZ * NY, NX, 96, T)
    attention, grad_proj, hidden_x = attention_call(projected, cotangent, hidden_t)
    grad_weight, grad_hidden = weight_call(grad_proj, hidden_x, weight)
    return attention, grad_hidden, grad_weight.transpose(1, 0, 2)


def solution(mesh):
    in_specs = (P("seq", None), P(None, None, "tp"), P("seq", "tp"))
    out_specs = (P("seq", "tp"), P("seq", "tp"), P("seq", None, "tp"))
    return jax.shard_map(
        on_device, mesh=mesh, in_specs=in_specs, out_specs=out_specs, check_vma=False
    )
```

```python
import math

import jax
import jax.numpy as jnp
from jax import lax
from jax.experimental import pallas as pl
from jax.experimental.pallas import tpu as pltpu
from jax.sharding import PartitionSpec as P

HD = 128
T = 256
NZ, NY, NX = 4, 2, 4
KEYS = NZ * NY * T
CHUNK = 512
SCALE = 1.0 / math.sqrt(HD)
LOG2 = SCALE * math.log2(math.e)
MESH = pl.DeviceIdType.MESH
F32, BF16 = jnp.float32, jnp.bfloat16
NN = (((1,), (0,)), ((), ()))
NT = (((1,), (1,)), ((), ()))


def dot(a, b, dims=NN):
    return lax.dot_general(a, b, dims, preferred_element_type=F32)


def coords():
    s = lax.axis_index("seq")
    return s // (NY * NX), (s // NX) % NY, s % NX, lax.axis_index("tp")


def seq_of(z, y, x):
    return (z * NY + y) * NX + x


def aligned(i, n):
    return pl.ds(pl.multiple_of(i * n, n), n)

Y_QG, Y_KVA, Y_KV1 = 0, 1, 2
X_QGA, X_QGR, X_QG1 = 3, 7, 11
Z_KVA, Z_KVAR, Z_KV1, Z_KV1R = 15, 19, 23, 27
X_HX, C_HX, X_STA, X_ST1 = 31, 35, 39, 43
X_GA0, X_GA1, X_GH = 47, 51, 55
C_DH, H_DH, N_SEM = 59, 61, 62
RING = (1, 2, 3)


def kernel(
    hidden_ref, w_ref, cot_ref, att_ref, dw_ref, dh_ref,
    h_v, w_v, cot_v, own_qg, own_kv, ht, hx, qg, kv, vkt, pt, ut, s_buf, st, sm, sm_all, ma, cs, es, rhs,
    ob, ro, kb, rk, gx_a, gx_h, dwb_a, dwr_a, dwb_h, dwr_h, dhb, dhc, dhs, dhr,
    sem_l, sem_s, sem_r, sem_os, sem_or, sem_ks, sem_kr, sem_ws, sem_wr,
):
    z, y, x, t = coords()
    other = 1 - y
    core = t % 2
    mate = t + 1 - 2 * core
    across = (t + 2) % 4
    me = lax.axis_index("seq")
    head_a, head_b = 2 * y, 2 - 2 * y
    zy = z * NY + y

    def at(zz, yy, xx):
        return (seq_of(zz, yy, xx), t)

    def xs(d):
        return (x + d) % NX

    def zs(d):
        return (z + d) % NZ

    local = [
        pltpu.make_async_copy(hidden_ref, h_v, sem_l.at[0]),
        pltpu.make_async_copy(w_ref.at[1], w_v.at[1], sem_l.at[1]),
        pltpu.make_async_copy(w_ref.at[2], w_v.at[2], sem_l.at[2]),
        pltpu.make_async_copy(w_ref.at[0], w_v.at[0], sem_l.at[3]),
        pltpu.make_async_copy(cot_ref, cot_v, sem_l.at[4]),
    ]
    for c in local:
        c.start()

    barrier = pltpu.get_barrier_semaphore()
    peers = [at(z, y, xs(d)) for d in RING] + [at(z, other, xs(d)) for d in range(4)]
    peers += [at(zs(d), y, x) for d in RING] + [at(zs(d), other, x) for d in RING]
    peers += [(me, mate), (me, across)]
    for peer in peers:
        pl.semaphore_signal(barrier, inc=1, device_id=peer, device_id_type=MESH)
    pl.semaphore_wait(barrier, len(peers))

    def remote(i, src, dst, peer):
        return pltpu.make_async_remote_copy(
            src_ref=src, dst_ref=dst, send_sem=sem_s.at[i], recv_sem=sem_r.at[i],
            device_id=peer, device_id_type=MESH,
        )

    sent = []

    def send(i, src, dst, peer):
        sent.append(remote(i, src, dst, peer))
        sent[-1].start()

    def got(i, dst):
        remote(i, dst, dst, (me, mate)).wait_recv()

    def qg_slot(yy, xx):
        return qg.at[4 + yy * NX + xx]

    def kv_rows(j, yy, zz):
        return kv.at[j, :, aligned(yy * NZ + zz, T), :]

    def columns(c, h):
        return w_v[c, :, aligned(h, HD)]

    def project_kv(h):
        v = dot(h_v[...], jnp.concatenate([columns(1, h), columns(2, h)], axis=1))
        own_kv[h, 0] = v[:, :HD].astype(BF16)
        own_kv[h, 1] = v[:, HD:].astype(BF16)

    partner = at(z, other, x)
    for c in local[:3]:
        c.wait()
    project_kv(head_b)
    send(Y_KVA, own_kv.at[head_b], kv_rows(1, y, z), partner)
    project_kv(head_a)
    for d in RING:
        send(Z_KVA + d, own_kv.at[head_a], kv_rows(1, y, z), at(zs(d), y, x))
    kv[1, :, aligned(y * NZ + z, T), :] = own_kv[head_a]
    for c in local[3:]:
        c.wait()
    for h in range(3):
        own_qg[h, 1] = cot_v[:, h * HD : (h + 1) * HD]
    v = dot(h_v[...], jnp.concatenate([columns(0, head_b), columns(0, head_a)], axis=1))
    own_qg[head_b, 0] = v[:, :HD].astype(BF16)
    own_qg[head_a, 0] = v[:, HD:].astype(BF16)
    send(Y_QG, own_qg.at[head_b], qg_slot(y, x), partner)
    for d in RING:
        send(X_QGA + d, own_qg.at[head_a], qg_slot(y, x), at(z, y, xs(d)))
    qg[4 + y * NX + x] = own_qg[head_a]

    got(Y_KVA, kv_rows(1, other, z))
    for d in RING:
        send(Z_KVAR + d, kv_rows(1, other, z), kv_rows(1, other, z), at(zs(d), y, x))
    project_kv(1)
    own_qg[1, 0] = dot(h_v[...], columns(0, 1)).astype(BF16)
    got(Y_QG, qg_slot(other, x))
    for d in RING:
        send(X_QGR + d, qg_slot(other, x), qg_slot(other, x), at(z, y, xs(d)))
    qg[x] = own_qg[1]
    kv[0, :, aligned(y * NZ + z, T), :] = own_kv[1]
    sm[...] = jnp.zeros_like(sm)
    ma[...] = jnp.zeros_like(ma)

    def hidden_rows(i, _):
        ht[i] = h_v[:, aligned(i, 384)].T.reshape(NX, 96, T)
        return 0

    lax.fori_loop(0, NZ * NY, hidden_rows, 0)
    hx[x] = ht[:, x]

    def transpose_block(j, yy, zz):
        i = yy * NZ + zz
        vkt[0:HD, aligned(i, T)] = kv[j, 1, aligned(i, T), :].T
        vkt[HD : 2 * HD, aligned(i, T)] = kv[j, 0, aligned(i, T), :].T

    def transpose_keys(j, base, base_relay):
        transpose_block(j, y, z)
        transpose_block(j, other, z)

        def step(d, _):
            got(base + d, kv_rows(j, y, zs(4 - d)))
            transpose_block(j, y, zs(4 - d))
            got(base_relay + d, kv_rows(j, other, zs(4 - d)))
            transpose_block(j, other, zs(4 - d))
            return 0

        lax.fori_loop(1, 4, step, 0)

    transpose_keys(1, Z_KVA, Z_KVAR)

    send(Y_KV1, own_kv.at[1], kv_rows(0, y, z), partner)
    half = pl.ds(4 * core, 4)
    for d in RING:
        send(Z_KV1 + d, own_kv.at[1], kv_rows(0, y, z), at(zs(d), y, x))
        send(X_HX + d, ht.at[half, xs(d)], hx.at[x, half], at(z, y, xs(d)))
    for d in RING:
        send(X_QG1 + d, own_qg.at[1], qg.at[x], at(z, y, xs(d)))

    chunks = [slice(c * CHUNK, (c + 1) * CHUNK) for c in range(KEYS // CHUNK)]

    def unit(j, q_slot, slot, row):
        q, g = qg[q_slot, 0], qg[q_slot, 1]
        top = None
        for c in chunks:
            s = dot(kv[j, 0, c, :], q, NT)
            s_buf[c] = s
            m = jnp.max(s, axis=0, keepdims=True)
            top = m if top is None else jnp.maximum(top, m)
        top = top * LOG2
        total, out = 0.0, 0.0
        for c in chunks:
            p = jnp.exp2(s_buf[c] * LOG2 - top)
            total = total + jnp.sum(p, axis=0, keepdims=True)
            p = p.astype(BF16)
            pt[slot, c, :] = p
            out = out + dot(vkt[:, c], p)
        g_t = g.astype(F32).T
        delta = jnp.sum(g_t * out[:HD], axis=0, keepdims=True) / total
        grad = 0.0
        for c in chunks:
            dp = dot(kv[j, 1, c, :], g, NT)
            d = (pt[slot, c, :].astype(F32) * (dp - delta)).astype(BF16)
            ut[slot, c, :] = d
            grad = grad + dot(vkt[HD:, c], d)
        st[slot, : 2 * HD] = out
        st[slot, 2 * HD :] = grad
        sm[j, 0, pl.ds(row, 1), :] = top + jnp.log2(total)
        sm[j, 1, pl.ds(row, 1), :] = delta
        ma[j, pl.ds(row, 1), :] = top

    def row_a(i):
        yy = (y + i // 4) % 2
        return yy, xs(4 - i % 4), yy * NX + xs(4 - i % 4)

    def relay_shared():
        rows = kv_rows(0, other, z)
        return [remote(Z_KV1R + d, rows, rows, at(zs(d), y, x)) for d in RING]

    def unit_a(i, _):
        _, _, r = row_a(i)

        @pl.when(i % 4 != 0)
        def _():
            got(X_QGA + i, qg.at[4 + r])

        @pl.when(i == 4)
        def _():
            got(Y_KV1, kv_rows(0, other, z))
            for c in relay_shared():
                c.start()

        unit(1, 4 + r, r, r)
        return 0

    lax.fori_loop(0, 8, unit_a, 0)
    sent.extend(relay_shared())

    def send_stats(j, base):
        for d in RING:
            send(base + d, sm.at[j], sm_all.at[j, x], at(z, y, xs(d)))
        sm_all[j, x] = sm[j]

    def combine(j, base):
        for d in RING:
            got(base + d, sm_all.at[j, xs(4 - d)])
        lse = sm_all[j, :, 0]
        top = jnp.max(lse, axis=0)
        lse_all = top + jnp.log2(jnp.sum(jnp.exp2(lse - top), axis=0))
        delta = jnp.sum(jnp.exp2(lse - lse_all) * sm_all[j, :, 1], axis=0)
        cs[j] = jnp.exp2(ma[j] - lse_all)
        es[j] = delta - sm[j, 1]

    send_stats(1, X_STA)
    for d in RING:
        part = hx.at[xs(4 - d), half]
        got(X_HX + d, part)
        send(C_HX + d, part, part, (me, mate))
    transpose_keys(0, Z_KV1, Z_KV1R)
    unit(0, x, 8, x)
    combine(1, X_STA)

    def prepare(j, row, slot, q_slot, r, b):
        c, e = cs[j, pl.ds(row, 1), :], es[j, pl.ds(row, 1), :]
        o = st[slot, 0:HD] * c
        dq = (st[slot, 2 * HD :] - e * st[slot, HD : 2 * HD]) * (c * SCALE)
        ob[b, 0] = o.T.astype(BF16)
        ob[b, 1] = dq.T.astype(BF16)
        cols = jnp.concatenate([c, e, jnp.zeros((6, T), F32)], axis=0).T
        c, e = cols[:, 0:1], cols[:, 1:2]
        cq = c * qg[q_slot, 0].astype(F32)
        rhs[r, :, 0:HD] = (c * qg[q_slot, 1].astype(F32)).astype(BF16)
        rhs[r, :, HD : 2 * HD] = (e * cq).astype(BF16)
        rhs[r, :, 2 * HD :] = cq.astype(BF16)

    def copy_o(kind, d, b, h, peer):
        return pltpu.make_async_remote_copy(
            src_ref=ob.at[b], dst_ref=ro.at[h, x], send_sem=sem_os.at[kind, d], recv_sem=sem_or.at[kind, d],
            device_id=peer, device_id_type=MESH,
        )

    def got_o(kind, d, h):
        pltpu.make_async_remote_copy(
            src_ref=ob.at[0], dst_ref=ro.at[h, xs(d)], send_sem=sem_os.at[kind, d], recv_sem=sem_or.at[kind, d],
            device_id=partner, device_id_type=MESH,
        ).wait_recv()

    def send_a(i):
        yy, xx, r = row_a(i)
        return copy_o(i // 4, i % 4, 4 + r, head_a, at(z, yy, xx))

    def prepare_a(k, _):
        i = 7 - k
        _, _, r = row_a(i)
        prepare(1, r, r, 4 + r, r, 4 + r)

        @pl.when(i != 0)
        def _():
            send_a(i).start()

        return 0

    lax.fori_loop(0, 8, prepare_a, 0)
    ro[head_a, x] = ob[4 + y * NX + x]

    def copy_k(j, own, d):
        yy = y if own else other
        zz = zs(d)
        kind = 2 * j + (0 if own else 1)
        b = j * 8 + yy * NZ + zz
        return pltpu.make_async_remote_copy(
            src_ref=kb.at[b], dst_ref=rk.at[j * 8 + y * NZ + z], send_sem=sem_ks.at[kind, d],
            recv_sem=sem_kr.at[kind, d], device_id=at(zz, yy, x), device_id_type=MESH,
        )

    def got_k(j, own, d):
        kind = 2 * j + (0 if own else 1)
        yy = y if own else other
        pltpu.make_async_remote_copy(
            src_ref=kb.at[0], dst_ref=rk.at[j * 8 + yy * NZ + zs(4 - d)], send_sem=sem_ks.at[kind, d],
            recv_sem=sem_kr.at[kind, d], device_id=partner, device_id_type=MESH,
        ).wait_recv()

    def key_block(j, i):
        slots = (8, 0, 1, 2) if j == 0 else range(8)
        rows = aligned(i, T)
        dv = dk = 0.0
        for r, slot in enumerate(slots):
            dv = dv + dot(pt[slot, rows, :], rhs[r, :, : 2 * HD])
            dk = dk + dot(ut[slot, rows, :], rhs[r, :, 2 * HD :])
        kb[j * 8 + i, 0] = ((dk - dv[:, HD:]) * SCALE).astype(BF16)
        kb[j * 8 + i, 1] = dv[:, :HD].astype(BF16)

    def loop(first, last, step):
        def body(i, _):
            step(i)
            return 0

        lax.fori_loop(first, last, body, 0)

    def key_blocks(j):
        def step(k):
            d = (k + 1) % 4
            yy = (other + k // 4) % 2
            key_block(j, yy * NZ + zs(d))

            @pl.when(k < 4)
            def _():
                copy_k(j, False, d).start()

            @pl.when((k >= 4) & (k < 7))
            def _():
                copy_k(j, True, d).start()

        loop(0, 8, step)
        rk[j * 8 + y * NZ + z] = kb[j * 8 + y * NZ + z]

    key_blocks(1)

    def unit_shared(d, _):
        got(X_QG1 + d, qg.at[xs(4 - d)])
        unit(0, xs(4 - d), d - 1, xs(4 - d))
        return 0

    lax.fori_loop(1, 4, unit_shared, 0)
    send_stats(0, X_ST1)

    def total_o(h, part):
        v = ro[h, 0, part].astype(F32)
        for xx in range(1, NX):
            v = v + ro[h, xx, part].astype(F32)
        return v.astype(BF16)

    def total_k(slots, part):
        v = 0.0
        for i in slots:
            v = v + rk[i, part].astype(F32)
        return v.astype(BF16)

    loop(1, 4, lambda d: got_o(0, d, head_a))
    loop(0, 4, lambda d: got_o(1, d, head_b))
    for i, h in enumerate((0, 2)):
        att_ref[:, h * HD : (h + 1) * HD] = total_o(h, 0)
        gx_a[x, 0, :, i * HD : (i + 1) * HD] = total_o(h, 1)
    for d in RING:
        send(X_GA0 + d, gx_a.at[x, 0], gx_a.at[x, 0], at(z, y, xs(d)))
    loop(1, 4, lambda d: got_k(1, True, d))
    loop(0, 4, lambda d: got_k(1, False, d))
    for i, slots in enumerate((range(8, 12), range(12, 16))):
        for part in (0, 1):
            gx_a[x, 1 + part, :, i * HD : (i + 1) * HD] = total_k(slots, part)
    for d in RING:
        send(X_GA1 + d, gx_a.at[x, pl.ds(1, 2)], gx_a.at[x, pl.ds(1, 2)], at(z, y, xs(d)))

    combine(0, X_ST1)

    def send_shared(d):
        return copy_o(2, d, xs(4 - d), 1, at(z, y, xs(4 - d)))

    def prepare_shared(d):
        slot = (d + 8) % 9
        prepare(0, xs(4 - d), slot, xs(4 - d), d, xs(4 - d))

        @pl.when(d != 0)
        def _():
            send_shared(d).start()

    loop(0, 4, prepare_shared)
    ro[1, x] = ob[x]
    key_blocks(0)

    def block(d):
        return (zy + d) % (NZ * NY)

    def copy_w(c, d):
        src, dst = (dwb_h.at[block(d)], dwr_h.at[zy]) if c == 3 else (dwb_a.at[block(d), c], dwr_a.at[zy, c])
        return pltpu.make_async_remote_copy(
            src_ref=src, dst_ref=dst, send_sem=sem_ws.at[c, d], recv_sem=sem_wr.at[c, d],
            device_id=(block(d) * NX + x, t), device_id_type=MESH,
        )

    def got_w(c, d):
        dst = dwr_h.at[block(8 - d)] if c == 3 else dwr_a.at[block(8 - d), c]
        pltpu.make_async_remote_copy(
            src_ref=dst, dst_ref=dst, send_sem=sem_ws.at[c, d], recv_sem=sem_wr.at[c, d],
            device_id=partner, device_id_type=MESH,
        ).wait_recv()

    def weight_rows(gx, dwb, c):
        def step(i):
            v = 0.0
            for xx in range(NX):
                v = v + dot(hx[xx, pl.ds(i * 4, 4)].reshape(4 * 96, T), gx[xx, c])
            dwb[pl.ds(i * 4, 4), c] = v.astype(BF16).reshape(4, 96, v.shape[1])

        loop(0, 2, step)

    for d in RING:
        got(C_HX + d, hx.at[xs(4 - d), pl.ds(4 - 4 * core, 4)])
        got(X_GA0 + d, gx_a.at[xs(4 - d), 0])
    for c in range(3):
        if c == 1:
            for d in RING:
                got(X_GA1 + d, gx_a.at[xs(4 - d), pl.ds(1, 2)])
        weight_rows(gx_a, dwb_a, c)
        loop(1, 8, lambda d, c=c: copy_w(c, d).start())
        dwr_a[zy, c] = dwb_a[zy, c]

    loop(1, 4, lambda d: got_o(2, d, 1))
    att_ref[:, HD : 2 * HD] = total_o(1, 0)
    gx_h[x, 0] = total_o(1, 1)
    loop(1, 4, lambda d: got_k(0, True, d))
    loop(0, 4, lambda d: got_k(0, False, d))
    for part in (0, 1):
        gx_h[x, 1 + part] = total_k(range(8), part)
    for d in RING:
        send(X_GH + d, gx_h.at[x], gx_h.at[x], at(z, y, xs(d)))

    def hidden_part(to):
        for i in range(3):
            v = 0.0
            for c in range(3):
                g = jnp.concatenate([gx_a[x, c, :, :HD], gx_h[x, c], gx_a[x, c, :, HD:]], axis=1)
                rows = pl.ds(pl.multiple_of(to * 768 + i * 256, 256), 256)
                v = v + dot(g, w_v[c, rows, :], NT)
            dhb[to, :, i * 256 : (i + 1) * 256] = v.astype(BF16)

    def hidden_mate(i):
        hidden_part(2 * i + 1 - core)
        copy_mate(i).start()

    def copy_mate(i):
        return remote(C_DH + i, dhb.at[2 * i + 1 - core], dhc.at[i], (me, mate))

    loop(0, 2, hidden_mate)
    loop(0, 2, lambda i: hidden_part(2 * i + core))
    for i in range(2):
        sent.append(copy_mate(i))
        got(C_DH + i, dhc.at[i])
    hi = t // 2
    dhs[...] = (dhb[across].astype(F32) + dhc[1 - hi].astype(F32)).astype(BF16)
    send(H_DH, dhs, dhr, (me, across))

    for d in RING:
        got(X_GH + d, gx_h.at[xs(4 - d)])
    for c in range(3):
        weight_rows(gx_h, dwb_h, c)
    loop(1, 8, lambda d: copy_w(3, d).start())
    dwr_h[zy] = dwb_h[zy]

    for c in range(3):
        loop(1, 8, lambda d, c=c: got_w(c, d))
        v = dwr_a[0, c].astype(F32)
        for i in range(1, 8):
            v = v + dwr_a[i, c].astype(F32)
        dw_ref[c, :, :HD] = v[:, :HD]
        dw_ref[c, :, 2 * HD :] = v[:, HD:]
    loop(1, 8, lambda d: got_w(3, d))
    for c in range(3):
        v = dwr_h[0, c].astype(F32)
        for i in range(1, 8):
            v = v + dwr_h[i, c].astype(F32)
        dw_ref[c, :, HD : 2 * HD] = v
    got(H_DH, dhr)
    dh_ref[...] = (dhb[t].astype(F32) + dhc[hi].astype(F32) + dhr[...].astype(F32)).astype(BF16)

    for c in sent:
        c.wait_send()
    loop(1, 8, lambda i: send_a(i).wait_send())
    loop(1, 4, lambda d: send_shared(d).wait_send())
    for j in (0, 1):
        loop(0, 4, lambda d, j=j: copy_k(j, False, d).wait_send())
        loop(1, 4, lambda d, j=j: copy_k(j, True, d).wait_send())
    for c in range(4):
        loop(1, 8, lambda d, c=c: copy_w(c, d).wait_send())


def call(hidden, weight, cotangent):
    block = (2, T, HD)
    scratch = [
        ((T, 3072), BF16),
        ((3, 3072, 384), BF16),
        ((T, 3 * HD), BF16),
        ((3,) + block, BF16),
        ((3,) + block, BF16),
        ((8, NX, 96, T), BF16),
        ((NX, 8, 96, T), BF16),
        ((12,) + block, BF16),
        ((2, 2, KEYS, HD), BF16),
        ((2 * HD, KEYS), BF16),
        ((9, KEYS, T), BF16),
        ((9, KEYS, T), BF16),
        ((KEYS, T), F32),
        ((9, 3 * HD, T), F32),
        ((2, 2, 8, T), F32),
        ((2, NX, 2, 8, T), F32),
        ((2, 8, T), F32),
        ((2, 8, T), F32),
        ((2, 8, T), F32),
        ((8, T, 3 * HD), BF16),
        ((12,) + block, BF16),
        ((3, NX) + block, BF16),
        ((16,) + block, BF16),
        ((16,) + block, BF16),
        ((NX, 3, T, 2 * HD), BF16),
        ((NX, 3, T, HD), BF16),
        ((8, 3, 96, 2 * HD), BF16),
        ((8, 3, 96, 2 * HD), BF16),
        ((8, 3, 96, HD), BF16),
        ((8, 3, 96, HD), BF16),
        ((4, T, 768), BF16),
        ((2, T, 768), BF16),
        ((T, 768), BF16),
        ((T, 768), BF16),
    ]
    sems = [(5,), (N_SEM,), (N_SEM,), (3, 4), (3, 4), (4, 4), (4, 4), (4, 8), (4, 8)]
    vmem = pl.BlockSpec(memory_space=pltpu.VMEM)
    hbm = pl.BlockSpec(memory_space=pl.ANY)
    return pl.pallas_call(
        kernel,
        out_shape=(
            jax.ShapeDtypeStruct((T, 3 * HD), BF16),
            jax.ShapeDtypeStruct((3, 96, 384), F32),
            jax.ShapeDtypeStruct((T, 768), BF16),
        ),
        in_specs=[hbm] * 3,
        out_specs=(vmem,) * 3,
        scratch_shapes=[pltpu.VMEM(*s) for s in scratch] + [pltpu.SemaphoreType.DMA(s) for s in sems],
        compiler_params=pltpu.CompilerParams(
            collective_id=0, has_side_effects=True, vmem_limit_bytes=63 * 2**20
        ),
        cost_estimate=pl.CostEstimate(flops=18 * 10**9, bytes_accessed=10**7, transcendentals=6 * 10**6),
        name="attention_with_gradients",
    )(hidden, weight, cotangent)


def on_device(hidden, qkv_weight, cotangent):
    attention, grad_weight, grad_hidden = call(hidden, qkv_weight.transpose(1, 0, 2), cotangent)
    return attention, grad_hidden, grad_weight.transpose(1, 0, 2)


def solution(mesh):
    in_specs = (P("seq", None), P(None, None, "tp"), P("seq", "tp"))
    out_specs = (P("seq", "tp"), P("seq", "tp"), P("seq", None, "tp"))
    return jax.shard_map(
        on_device, mesh=mesh, in_specs=in_specs, out_specs=out_specs, check_vma=False
    )
```

```python
import math

import jax
import jax.numpy as jnp
from jax import lax
from jax.experimental import pallas as pl
from jax.experimental.pallas import tpu as pltpu
from jax.sharding import PartitionSpec as P

HD = 128
T = 256
NZ, NY, NX = 4, 2, 4
KEYS = NZ * NY * T
CHUNK = 512
SCALE = 1.0 / math.sqrt(HD)
LOG2 = SCALE * math.log2(math.e)
MESH = pl.DeviceIdType.MESH
F32, BF16 = jnp.float32, jnp.bfloat16
NN = (((1,), (0,)), ((), ()))
NT = (((1,), (1,)), ((), ()))


def dot(a, b, dims=NN):
    return lax.dot_general(a, b, dims, preferred_element_type=F32)


def coords():
    s = lax.axis_index("seq")
    return s // (NY * NX), (s // NX) % NY, s % NX, lax.axis_index("tp")


def seq_of(z, y, x):
    return (z * NY + y) * NX + x


def aligned(i, n):
    return pl.ds(pl.multiple_of(i * n, n), n)

Y_QG, Y_KVA, Y_KV1 = 0, 1, 2
X_QGA, X_QGR, X_QG1 = 3, 7, 11
Z_KVA, Z_KVAR, Z_KV1, Z_KV1R = 15, 19, 23, 27
X_HX, C_HX, X_STA, X_ST1 = 31, 35, 39, 43
X_GA, X_GHV, X_GHK, X_GHQ = 47, 51, 55, 67
C_DH, H_DH = 59, 61
Y_OA, Y_KA, Y_V1, Y_K1, Y_WA, Y_W1 = 62, 63, 64, 65, 66, 67
X_GB, X_GC, X_GD, N_SEM = 71, 75, 79, 83
RING = (1, 2, 3)


def kernel(
    hidden_ref, w_ref, cot_ref, att_ref, dw_ref, dh_ref,
    h_v, w_v, cot_v, far_qg, far_kv, ht, hx, qg, kv, vkt, pt, ut, s_buf, top_buf, st, sm, sm_all, ma, cs, es, rhs,
    ob, ro, kb, rk, ya_s, ya_r, y1_s, y1_r, ywa_s, ywa_r, yw1_s, yw1_r,
    gx_a, gx_h, dwb_a, dwr_a, dwb_h, dwr_h, dhc, dhr,
    sem_l, sem_s, sem_r, sem_os, sem_or, sem_ks, sem_kr, sem_ws, sem_wr,
):
    z, y, x, t = coords()
    other = 1 - y
    core = t % 2
    mate = t + 1 - 2 * core
    across = (t + 2) % 4
    me = lax.axis_index("seq")
    head_a, head_b = 2 * y, 2 - 2 * y

    def at(zz, yy, xx):
        return (seq_of(zz, yy, xx), t)

    def xs(d):
        return (x + d) % NX

    def zs(d):
        return (z + d) % NZ

    local = [
        pltpu.make_async_copy(hidden_ref, h_v, sem_l.at[0]),
        pltpu.make_async_copy(w_ref.at[1], w_v.at[1], sem_l.at[1]),
        pltpu.make_async_copy(w_ref.at[2], w_v.at[2], sem_l.at[2]),
        pltpu.make_async_copy(w_ref.at[0], w_v.at[0], sem_l.at[3]),
        pltpu.make_async_copy(cot_ref, cot_v, sem_l.at[4]),
    ]
    for c in local:
        c.start()

    barrier = pltpu.get_barrier_semaphore()
    peers = [at(z, y, xs(d)) for d in RING] + [at(zs(d), y, x) for d in RING]
    peers += [at(z, other, x), (me, mate), (me, across)]
    for peer in peers:
        pl.semaphore_signal(barrier, inc=1, device_id=peer, device_id_type=MESH)
    pl.semaphore_wait(barrier, len(peers))

    def remote(i, src, dst, peer):
        return pltpu.make_async_remote_copy(
            src_ref=src, dst_ref=dst, send_sem=sem_s.at[i], recv_sem=sem_r.at[i],
            device_id=peer, device_id_type=MESH,
        )

    sent = []

    def send(i, src, dst, peer):
        sent.append(remote(i, src, dst, peer))
        sent[-1].start()

    def got(i, dst):
        remote(i, dst, dst, (me, mate)).wait_recv()

    def qg_slot(yy, xx):
        return qg.at[4 + yy * NX + xx]

    def kv_rows(j, yy, zz):
        return kv.at[j, :, aligned(yy * NZ + zz, T), :]

    def columns(c, h):
        return w_v[c, :, aligned(h, HD)]

    def project_kv(h, dst):
        v = dot(h_v[...], jnp.concatenate([columns(1, h), columns(2, h)], axis=1))
        dst[0] = v[:, :HD].astype(BF16)
        dst[1] = v[:, HD:].astype(BF16)

    partner = at(z, other, x)
    own_a, own_1 = qg_slot(y, x), qg.at[x]
    keys_a, keys_1 = kv_rows(1, y, z), kv_rows(0, y, z)
    for c in local[:3]:
        c.wait()
    project_kv(head_b, far_kv)
    send(Y_KVA, far_kv, keys_a, partner)
    project_kv(head_a, keys_a)
    for d in (2, 1, 3):
        send(Z_KVA + d, keys_a, keys_a, at(zs(d), y, x))
    for c in local[3:]:
        c.wait()
    own_1[1] = cot_v[:, HD : 2 * HD]
    own_a[1] = cot_v[:, aligned(head_a, HD)]
    far_qg[1] = cot_v[:, aligned(head_b, HD)]
    v = dot(h_v[...], jnp.concatenate([columns(0, head_b), columns(0, head_a)], axis=1))
    far_qg[0] = v[:, :HD].astype(BF16)
    own_a[0] = v[:, HD:].astype(BF16)
    send(Y_QG, far_qg, own_a, partner)
    for d in (2, 1, 3):
        send(X_QGA + d, own_a, own_a, at(z, y, xs(d)))

    got(Y_KVA, kv_rows(1, other, z))
    for d in (2, 1, 3):
        send(Z_KVAR + d, kv_rows(1, other, z), kv_rows(1, other, z), at(zs(d), y, x))
    project_kv(1, keys_1)
    own_1[0] = dot(h_v[...], columns(0, 1)).astype(BF16)
    got(Y_QG, qg_slot(other, x))
    for d in (2, 1, 3):
        send(X_QGR + d, qg_slot(other, x), qg_slot(other, x), at(z, y, xs(d)))
    sm[...] = jnp.zeros_like(sm)
    ma[...] = jnp.zeros_like(ma)

    def hidden_rows(i, _):
        ht[i] = h_v[:, aligned(i, 384)].T.reshape(NX, 96, T)
        return 0

    lax.fori_loop(0, NZ * NY, hidden_rows, 0)
    hx[x] = ht[:, x]

    def transpose_block(j, yy, zz):
        i = yy * NZ + zz
        vkt[0:HD, aligned(i, T)] = kv[j, 1, aligned(i, T), :].T
        vkt[HD : 2 * HD, aligned(i, T)] = kv[j, 0, aligned(i, T), :].T

    def transpose_keys(j, base, base_relay):
        def step(d, _):
            zz = zs(4 - d)
            if base is not None:

                @pl.when(d != 0)
                def _():
                    got(base + d, kv_rows(j, y, zz))
                    got(base_relay + d, kv_rows(j, other, zz))

            transpose_block(j, y, zz)
            transpose_block(j, other, zz)
            return 0

        lax.fori_loop(0, 4, step, 0)

    transpose_keys(1, Z_KVA, Z_KVAR)

    send(Y_KV1, keys_1, keys_1, partner)
    half = pl.ds(4 * core, 4)
    rows_sent = []
    for d in (2, 1, 3):
        send(Z_KV1 + d, keys_1, keys_1, at(zs(d), y, x))
        rows_sent.append(remote(X_HX + d, ht.at[half, xs(d)], hx.at[x, half], at(z, y, xs(d))))
        rows_sent[-1].start()
    for d in RING:
        send(X_QG1 + d, own_1, own_1, at(z, y, xs(d)))

    chunks = [slice(c * CHUNK, (c + 1) * CHUNK) for c in range(KEYS // CHUNK)]

    def scores(j, q_slot, c, top):
        s = dot(kv[j, 0, c, :], qg[q_slot, 0], NT)
        s_buf[c] = s
        return jnp.maximum(top, jnp.max(s, axis=0, keepdims=True))

    least = jnp.full((1, T), -jnp.inf, F32)

    def unit(j, q_slot, slot, row, following):
        g = qg[q_slot, 1]
        top = top_buf[0:1] * LOG2
        total, out = 0.0, 0.0
        for c in chunks:
            p = jnp.exp2(s_buf[c] * LOG2 - top)
            total = total + jnp.sum(p, axis=0, keepdims=True)
            p = p.astype(BF16)
            pt[slot, c, :] = p
            out = out + dot(vkt[:, c], p)
        g_t = g.astype(F32).T
        delta = jnp.sum(g_t * out[:HD], axis=0, keepdims=True) / total
        grad, top_next = 0.0, least
        for c in chunks:
            if following is not None:
                top_next = scores(*following, c, top_next)
            dp = dot(kv[j, 1, c, :], g, NT)
            d = (pt[slot, c, :].astype(F32) * (dp - delta)).astype(BF16)
            ut[slot, c, :] = d
            grad = grad + dot(vkt[HD:, c], d)
        st[slot, : 2 * HD] = out
        st[slot, 2 * HD :] = grad
        sm[j, 0, pl.ds(row, 1), :] = top + jnp.log2(total)
        sm[j, 1, pl.ds(row, 1), :] = delta
        ma[j, pl.ds(row, 1), :] = top
        top_buf[0:1] = top_next

    def row_a(i):
        yy = (y + i // 4) % 2
        return yy, xs(4 - i % 4), yy * NX + xs(4 - i % 4)

    def relay_shared():
        rows = kv_rows(0, other, z)
        return [remote(Z_KV1R + d, rows, rows, at(zs(d), y, x)) for d in (1, 3)]

    def cross_shared():
        rows = kv_rows(0, y, zs(2))
        return remote(Z_KV1R + 2, rows, rows, partner)

    def unit_a(i, _):
        _, _, r = row_a(i)
        _, _, r_next = row_a(i + 1)

        @pl.when((i != 3) & (i != 7))
        def _():
            got(X_QGA + i + 1, qg.at[4 + r_next])

        @pl.when(i == 3)
        def _():
            got(Y_KV1, kv_rows(0, other, z))
            for c in relay_shared():
                c.start()
            got(Z_KV1 + 2, kv_rows(0, y, zs(2)))
            cross_shared().start()

        @pl.when(i == 7)
        def _():
            for d in (1, 3):
                got(Z_KV1 + d, kv_rows(0, y, zs(4 - d)))
            for d in RING:
                got(Z_KV1R + d, kv_rows(0, other, zs(4 - d)))

        last = i // 7
        unit(1, 4 + r, r, r, (1 - last, jnp.where(last == 1, x, 4 + r_next)))
        return 0

    top = least
    for c in chunks:
        top = scores(1, 4 + y * NX + x, c, top)
    top_buf[0:1] = top
    lax.fori_loop(0, 8, unit_a, 0)
    sent.extend(relay_shared() + [cross_shared()])

    def send_stats(j, base):
        for d in RING:
            send(base + d, sm.at[j], sm_all.at[j, x], at(z, y, xs(d)))
        sm_all[j, x] = sm[j]

    def combine(j, base):
        for d in RING:
            got(base + d, sm_all.at[j, xs(4 - d)])
        lse = sm_all[j, :, 0]
        top = jnp.max(lse, axis=0)
        lse_all = top + jnp.log2(jnp.sum(jnp.exp2(lse - top), axis=0))
        delta = jnp.sum(jnp.exp2(lse - lse_all) * sm_all[j, :, 1], axis=0)
        cs[j] = jnp.exp2(ma[j] - lse_all)
        es[j] = delta - sm[j, 1]

    send_stats(1, X_STA)
    for d in RING:
        part = hx.at[xs(4 - d), half]
        got(X_HX + d, part)
        send(C_HX + d, part, part, (me, mate))
    transpose_keys(0, None, None)
    got(X_QG1 + 1, qg.at[xs(3)])
    unit(0, x, 8, x, (0, xs(3)))
    combine(1, X_STA)

    def prepare(j, row, slot, q_slot, r, b):
        c, e = cs[j, pl.ds(row, 1), :], es[j, pl.ds(row, 1), :]
        o = st[slot, 0:HD] * c
        dq = (st[slot, 2 * HD :] - e * st[slot, HD : 2 * HD]) * (c * SCALE)
        ob[b, 0] = o.T.astype(BF16)
        ob[b, 1] = dq.T.astype(BF16)
        cols = jnp.concatenate([c, e, jnp.zeros((6, T), F32)], axis=0).T
        c, e = cols[:, 0:1], cols[:, 1:2]
        cq = c * qg[q_slot, 0].astype(F32)
        rhs[r, :, 0:HD] = (c * qg[q_slot, 1].astype(F32)).astype(BF16)
        rhs[r, :, HD : 2 * HD] = (e * cq).astype(BF16)
        rhs[r, :, 2 * HD :] = cq.astype(BF16)

    def copy_o(kind, d, b):
        return pltpu.make_async_remote_copy(
            src_ref=ob.at[b], dst_ref=ro.at[kind, x], send_sem=sem_os.at[kind, d], recv_sem=sem_or.at[kind, d],
            device_id=at(z, y, xs(4 - d)), device_id_type=MESH,
        )

    def got_o(kind):
        def step(d):
            dst = ro.at[kind, xs(d)]
            pltpu.make_async_remote_copy(
                src_ref=dst, dst_ref=dst, send_sem=sem_os.at[kind, d], recv_sem=sem_or.at[kind, d],
                device_id=partner, device_id_type=MESH,
            ).wait_recv()

        loop(1, 4, step)

    def send_a(i):
        return copy_o(i // 4, i % 4, row_a(i)[2])

    def loop(first, last, step):
        def body(i, _):
            step(i)
            return 0

        lax.fori_loop(first, last, body, 0)

    def prepare_a(k):
        i = 7 - k
        _, _, r = row_a(i)
        prepare(1, r, r, 4 + r, r, r)

        @pl.when(i % 4 != 0)
        def _():
            send_a(i).start()

    loop(0, 8, prepare_a)
    ro[0, x] = ob[y * NX + x]
    ro[1, x] = ob[other * NX + x]

    def k_block(row, zz):
        return ((y + row) % 2) * NZ + zz

    def k_part(kind):
        return pl.ds(0, 2) if kind < 2 else pl.ds(1, 1) if kind < 4 else pl.ds(0, 1)

    def k_slots(kind):
        return (2 if kind < 2 else 0) + kind % 2

    def copy_k(kind, d):
        src = kb.at[k_block(kind % 2, zs(d)), k_part(kind)]
        return pltpu.make_async_remote_copy(
            src_ref=src, dst_ref=rk.at[k_slots(kind), z, k_part(kind)], send_sem=sem_ks.at[kind, d],
            recv_sem=sem_kr.at[kind, d], device_id=at(zs(d), y, x), device_id_type=MESH,
        )

    def got_k(kind):
        def step(d):
            dst = rk.at[k_slots(kind), zs(4 - d), k_part(kind)]
            pltpu.make_async_remote_copy(
                src_ref=dst, dst_ref=dst, send_sem=sem_ks.at[kind, d],
                recv_sem=sem_kr.at[kind, d], device_id=partner, device_id_type=MESH,
            ).wait_recv()

        loop(1, 4, step)

    def key_blocks(step, kind):
        for row in (1, 0):

            def one(k, row=row):
                zz = 2 * ((z // 2 + 1 + k) % 2)
                b = k_block(row, zz)
                step(b)
                for i in (0, 1):
                    d = (zz + i + NZ - z) % NZ

                    @pl.when(d != 0)
                    def _():
                        copy_k(kind + row, d).start()

            loop(0, 2, one)
            b, part = k_block(row, z), k_part(kind)
            rk[k_slots(kind + row), z, part] = kb[b, part]

    def two_rows(i):
        return pl.ds(pl.multiple_of(i * T, 2 * T), 2 * T)

    def put(b, part, v):
        kb[b, part] = v[:T].astype(BF16)
        kb[b + 1, part] = v[T:].astype(BF16)

    def block_a(i):
        dv = dk = 0.0
        for r in range(8):
            dv = dv + dot(pt[r, two_rows(i), :], rhs[r, :, : 2 * HD])
            dk = dk + dot(ut[r, two_rows(i), :], rhs[r, :, 2 * HD :])
        put(i, 0, (dk - dv[:, HD:]) * SCALE)
        put(i, 1, dv[:, :HD])

    shared_slots = (8, 0, 1, 2)

    def block_v(i):
        dv = 0.0
        for r, slot in enumerate(shared_slots):
            dv = dv + dot(pt[slot, two_rows(i), :], rhs[r, :, : 2 * HD])
        st[i, : 2 * HD, :HD] = dv[:T, HD:]
        st[i + 1, : 2 * HD, :HD] = dv[T:, HD:]
        put(i, 1, dv[:, :HD])

    def block_k(i):
        dk = 0.0
        for r, slot in enumerate(shared_slots):
            dk = dk + dot(ut[slot, two_rows(i), :], rhs[r, :, 2 * HD :])
        put(i, 0, (dk - jnp.concatenate([st[i, : 2 * HD, :HD], st[i + 1, : 2 * HD, :HD]], axis=0)) * SCALE)

    key_blocks(block_a, 0)

    def total(ref, kind, part):
        v = ref[kind, 0, part].astype(F32)
        for i in range(1, 4):
            v = v + ref[kind, i, part].astype(F32)
        return v

    mine, theirs = aligned(y, HD), aligned(other, HD)
    q_part, kv_part = pl.ds(0, 1), pl.ds(1, 2)

    def piece_a(d, part, cols):
        return gx_a.at[xs(d), part, :, cols]

    def gather_a(base, part, cols):
        piece = piece_a(0, part, cols)
        return [remote(base + d, piece, piece, at(z, y, xs(d))) for d in (1, 3)]

    def pass_on(base, part, cols, step):
        piece = piece_a(4 - step, part, cols)
        return remote(base + 2, piece, piece, at(z, y, xs(step)))

    def forward_a(base, part, cols, step):
        got(base + step, piece_a(4 - step, part, cols))
        pass_on(base, part, cols, step).start()

    pieces = {X_GA: (q_part, mine, 1), X_GB: (q_part, theirs, 3), X_GC: (kv_part, mine, 1), X_GD: (kv_part, theirs, 3)}

    def got_a(base):
        part, cols, step = pieces[base]
        got(base + 4 - step, piece_a(step, part, cols))
        got(base + 2, piece_a(2, part, cols))

    def far_o():
        return remote(Y_OA, ya_s.at[pl.ds(0, 2)], ya_r.at[pl.ds(0, 2)], partner)

    def far_k():
        return remote(Y_KA, ya_s.at[pl.ds(2, 2)], ya_r.at[pl.ds(2, 2)], partner)

    def start_all(copies):
        for c in copies:
            c.start()

    def unit_shared(d):
        got(X_QG1 + d + 1, qg.at[xs(3 - d)])
        unit(0, xs(4 - d), d - 1, xs(4 - d), (0, xs(3 - d)))

        @pl.when(d == 1)
        def _():
            got_o(1)
            for part in (0, 1):
                ya_s[part] = total(ro, 1, part).astype(BF16)
            far_o().start()
            got_o(0)
            att_ref[:, aligned(head_a, HD)] = total(ro, 0, 0).astype(BF16)
            gx_a[x, 0, :, mine] = total(ro, 0, 1).astype(BF16)
            start_all(gather_a(X_GA, q_part, mine))

        @pl.when(d == 2)
        def _():
            got_k(1)
            for part in (0, 1):
                ya_s[2 + part] = total(rk, 3, part).astype(BF16)
            far_k().start()
            got(Y_OA, ya_r.at[pl.ds(0, 2)])
            att_ref[:, aligned(head_b, HD)] = ya_r[0]
            gx_a[x, 0, :, theirs] = ya_r[1]
            start_all(gather_a(X_GB, q_part, theirs))
            got_k(0)
            for part in (0, 1):
                gx_a[x, 1 + part, :, mine] = total(rk, 2, part).astype(BF16)
            start_all(gather_a(X_GC, kv_part, mine))
            forward_a(X_GA, q_part, mine, 1)

    loop(1, 3, unit_shared)
    unit(0, xs(1), 2, xs(1), None)
    send_stats(0, X_ST1)
    got(Y_KA, ya_r.at[pl.ds(2, 2)])
    for c in (1, 2):
        gx_a[x, c, :, theirs] = ya_r[1 + c]
    start_all(gather_a(X_GD, kv_part, theirs))
    sent.extend([far_o(), far_k()])
    forward_a(X_GB, q_part, theirs, 3)
    for base, (part, cols, step) in pieces.items():
        sent.extend(gather_a(base, part, cols))
        sent.append(pass_on(base, part, cols, step))

    combine(0, X_ST1)

    def send_shared(d):
        return copy_o(2, d, xs(4 - d))

    def prepare_shared(d):
        slot = (d + 8) % 9
        prepare(0, xs(4 - d), slot, xs(4 - d), d, xs(4 - d))

        @pl.when(d != 0)
        def _():
            send_shared(d).start()

    for c in range(2):
        loop(1, 4, lambda d, c=c: send_a(4 * c + d).wait_send())
    loop(0, 4, prepare_shared)
    ro[2, x] = ob[x]

    forward_a(X_GC, kv_part, mine, 1)
    for kind in (0, 1):
        loop(1, 4, lambda d, kind=kind: copy_k(kind, d).wait_send())
    key_blocks(block_v, 2)
    forward_a(X_GD, kv_part, theirs, 3)
    key_blocks(block_k, 4)

    def copy_w(c, d):
        ref, dst = (dwb_h, dwr_h) if c >= 3 else (dwb_a, dwr_a)
        return pltpu.make_async_remote_copy(
            src_ref=ref.at[zs(d), c % 3], dst_ref=dst.at[z, c % 3], send_sem=sem_ws.at[c, d],
            recv_sem=sem_wr.at[c, d], device_id=at(zs(d), y, x), device_id_type=MESH,
        )

    def got_w(c):
        def step(d):
            dst = (dwr_h if c >= 3 else dwr_a).at[zs(4 - d), c % 3]
            pltpu.make_async_remote_copy(
                src_ref=dst, dst_ref=dst, send_sem=sem_ws.at[c, d], recv_sem=sem_wr.at[c, d],
                device_id=partner, device_id_type=MESH,
            ).wait_recv()

        loop(1, 4, step)

    def weight_rows(c):
        gx, dwb, dwr = (gx_h, dwb_h, dwr_h) if c >= 3 else (gx_a, dwb_a, dwr_a)

        def step(i):
            v = 0.0
            for xx in range(NX):
                v = v + dot(hx[xx, pl.ds(i * 4, 4)].reshape(4 * 96, T), gx[xx, c % 3])
            dwb[pl.ds(i * 2, 2), c % 3] = v.astype(BF16).reshape(2, 2, 96, v.shape[1])

        loop(0, 2, step)
        loop(1, 4, lambda d: copy_w(c, d).start())
        dwr[z, c % 3] = dwb[z, c % 3]

    got_o(2)
    att_ref[:, HD : 2 * HD] = total(ro, 2, 0).astype(BF16)
    gx_h[x, 0] = total(ro, 2, 1).astype(BF16)
    for d in RING:
        send(X_GHQ + d, gx_h.at[x, 0], gx_h.at[x, 0], at(z, y, xs(d)))
    got_k(3)
    y1_s[1] = total(rk, 1, 1).astype(BF16)
    send(Y_V1, y1_s.at[1], y1_r.at[1], partner)

    for d in RING:
        got(C_HX + d, hx.at[xs(4 - d), pl.ds(4 - 4 * core, 4)])
    got_a(X_GA)
    got_a(X_GB)
    weight_rows(0)

    got_k(2)
    got(Y_V1, y1_r.at[1])
    gx_h[x, 2] = (total(rk, 0, 1) + y1_r[1].astype(F32)).astype(BF16)
    for d in RING:
        send(X_GHV + d, gx_h.at[x, 2], gx_h.at[x, 2], at(z, y, xs(d)))
    got_a(X_GC)
    got_a(X_GD)
    weight_rows(1)
    got_k(5)
    y1_s[0] = total(rk, 1, 0).astype(BF16)
    send(Y_K1, y1_s.at[0], y1_r.at[0], partner)
    weight_rows(2)
    got_k(4)
    got(Y_K1, y1_r.at[0])
    gx_h[x, 1] = (total(rk, 0, 0) + y1_r[0].astype(F32)).astype(BF16)
    for d in RING:
        send(X_GHK + d, gx_h.at[x, 1], gx_h.at[x, 1], at(z, y, xs(d)))

    for c in rows_sent:
        c.wait_send()

    def part_of(to):
        return ht.at[pl.ds(2 * to, 2)]

    def hidden_part(to):
        pieces = []
        for i in range(3):
            v = 0.0
            for c in range(3):
                g = jnp.concatenate([gx_a[x, c, :, :HD], gx_h[x, c], gx_a[x, c, :, HD:]], axis=1)
                rows = pl.ds(pl.multiple_of(to * 768 + i * 256, 256), 256)
                v = v + dot(g, w_v[c, rows, :], NT)
            pieces.append(v.astype(BF16))
        part_of(to)[...] = jnp.concatenate(pieces, axis=0).reshape(2, NX, 96, T)

    def hidden_mate(i):
        hidden_part(2 * i + 1 - core)
        copy_mate(i).start()

    def copy_mate(i):
        return remote(C_DH + i, part_of(2 * i + 1 - core), dhc.at[i], (me, mate))

    loop(0, 2, hidden_mate)
    loop(0, 2, lambda i: hidden_part(2 * i + core))
    for i in range(2):
        sent.append(copy_mate(i))
        got(C_DH + i, dhc.at[i])
    hi = t // 2
    far = part_of(across)
    far[...] = (far[...].astype(F32) + dhc[1 - hi].astype(F32)).astype(BF16)
    send(H_DH, far, dhr, (me, across))

    for c, base in ((0, X_GHQ), (2, X_GHV), (1, X_GHK)):
        for d in RING:
            got(base + d, gx_h.at[xs(4 - d), c])
        weight_rows(3 + c)

    def total_w(ref, c, row):
        v = ref[0, c, row].astype(F32)
        for i in range(1, NZ):
            v = v + ref[i, c, row].astype(F32)
        return v

    for c in range(3):
        got_w(c)
        ywa_s[c] = total_w(dwr_a, c, other).astype(BF16)
    send(Y_WA, ywa_s, ywa_r, partner)
    for c in range(3):
        got_w(3 + c)
        yw1_s[c] = total_w(dwr_h, c, other).astype(BF16)
    send(Y_W1, yw1_s, yw1_r, partner)
    got(Y_WA, ywa_r)
    for c in range(3):
        v = total_w(dwr_a, c, y) + ywa_r[c].astype(F32)
        dw_ref[c, :, :HD] = v[:, :HD]
        dw_ref[c, :, 2 * HD :] = v[:, HD:]
    got(Y_W1, yw1_r)
    for c in range(3):
        dw_ref[c, :, HD : 2 * HD] = total_w(dwr_h, c, y) + yw1_r[c].astype(F32)
    got(H_DH, dhr)
    v = (part_of(t)[...].astype(F32) + dhc[hi].astype(F32) + dhr[...].astype(F32)).astype(BF16).reshape(3 * T, T)
    for i in range(3):
        dh_ref[:, i * T : (i + 1) * T] = v[i * T : (i + 1) * T]

    for c in sent:
        c.wait_send()
    loop(1, 4, lambda d: send_shared(d).wait_send())
    for kind in range(6):
        if kind > 1:
            loop(1, 4, lambda d, kind=kind: copy_k(kind, d).wait_send())
        loop(1, 4, lambda d, c=kind: copy_w(c, d).wait_send())


def call(hidden, weight, cotangent):
    block = (2, T, HD)
    scratch = [
        ((T, 3072), BF16),
        ((3, 3072, 384), BF16),
        ((T, 3 * HD), BF16),
        (block, BF16),
        (block, BF16),
        ((8, NX, 96, T), BF16),
        ((NX, 8, 96, T), BF16),
        ((12,) + block, BF16),
        ((2, 2, KEYS, HD), BF16),
        ((2 * HD, KEYS), BF16),
        ((9, KEYS, T), BF16),
        ((9, KEYS, T), BF16),
        ((KEYS, T), F32),
        ((8, T), F32),
        ((9, 3 * HD, T), F32),
        ((2, 2, 8, T), F32),
        ((2, NX, 2, 8, T), F32),
        ((2, 8, T), F32),
        ((2, 8, T), F32),
        ((2, 8, T), F32),
        ((8, T, 3 * HD), BF16),
        ((8,) + block, BF16),
        ((3, NX) + block, BF16),
        ((8,) + block, BF16),
        ((4, NZ) + block, BF16),
        ((4, T, HD), BF16),
        ((4, T, HD), BF16),
        (block, BF16),
        (block, BF16),
        ((3, 96, 2 * HD), BF16),
        ((3, 96, 2 * HD), BF16),
        ((3, 96, HD), BF16),
        ((3, 96, HD), BF16),
        ((NX, 3, T, 2 * HD), BF16),
        ((NX, 3, T, HD), BF16),
        ((NZ, 3, 2, 96, 2 * HD), BF16),
        ((NZ, 3, 2, 96, 2 * HD), BF16),
        ((NZ, 3, 2, 96, HD), BF16),
        ((NZ, 3, 2, 96, HD), BF16),
        ((2, 2, NX, 96, T), BF16),
        ((2, NX, 96, T), BF16),
    ]
    sems = [(5,), (N_SEM,), (N_SEM,), (3, 4), (3, 4), (6, 4), (6, 4), (6, 4), (6, 4)]
    vmem = pl.BlockSpec(memory_space=pltpu.VMEM)
    hbm = pl.BlockSpec(memory_space=pl.ANY)
    return pl.pallas_call(
        kernel,
        out_shape=(
            jax.ShapeDtypeStruct((T, 3 * HD), BF16),
            jax.ShapeDtypeStruct((3, 96, 384), F32),
            jax.ShapeDtypeStruct((T, 768), BF16),
        ),
        in_specs=[hbm] * 3,
        out_specs=(vmem,) * 3,
        scratch_shapes=[pltpu.VMEM(*s) for s in scratch] + [pltpu.SemaphoreType.DMA(s) for s in sems],
        compiler_params=pltpu.CompilerParams(
            collective_id=0, has_side_effects=True, vmem_limit_bytes=63 * 2**20
        ),
        cost_estimate=pl.CostEstimate(flops=18 * 10**9, bytes_accessed=10**7, transcendentals=6 * 10**6),
        name="attention_with_gradients",
    )(hidden, weight, cotangent)


def copy_kernel(*refs):
    for src, dst in zip(refs[:3], refs[3:]):
        dst[...] = src[...]


def copy_out(arrays):
    vmem = pl.BlockSpec(memory_space=pltpu.VMEM)
    return pl.pallas_call(
        copy_kernel,
        out_shape=tuple(jax.ShapeDtypeStruct(a.shape, a.dtype) for a in arrays),
        in_specs=[vmem] * 3,
        out_specs=(vmem,) * 3,
        name="copy_out",
    )(*arrays)


def on_device(hidden, qkv_weight, cotangent):
    arrays = call(hidden, qkv_weight.transpose(1, 0, 2), cotangent)
    attention, grad_weight, grad_hidden = copy_out(arrays)
    return attention, grad_hidden, grad_weight.transpose(1, 0, 2)


def solution(mesh):
    in_specs = (P("seq", None), P(None, None, "tp"), P("seq", "tp"))
    out_specs = (P("seq", "tp"), P("seq", "tp"), P("seq", None, "tp"))
    return jax.shard_map(
        on_device, mesh=mesh, in_specs=in_specs, out_specs=out_specs, check_vma=False
    )
```

```python
import math

import jax
import jax.numpy as jnp
from jax import lax
from jax.experimental import pallas as pl
from jax.experimental.pallas import tpu as pltpu
from jax.sharding import PartitionSpec as P

HD = 128
T = 256
NZ, NY, NX = 4, 2, 4
KEYS = NZ * NY * T
CHUNK = 512
SCALE = 1.0 / math.sqrt(HD)
LOG2 = SCALE * math.log2(math.e)
MESH = pl.DeviceIdType.MESH
F32, BF16 = jnp.float32, jnp.bfloat16
NN = (((1,), (0,)), ((), ()))
NT = (((1,), (1,)), ((), ()))


def dot(a, b, dims=NN):
    return lax.dot_general(a, b, dims, preferred_element_type=F32)


def coords():
    s = lax.axis_index("seq")
    return s // (NY * NX), (s // NX) % NY, s % NX, lax.axis_index("tp")


def seq_of(z, y, x):
    return (z * NY + y) * NX + x


def aligned(i, n):
    return pl.ds(pl.multiple_of(i * n, n), n)

Y_QG, Y_KVA, Y_KV1 = 0, 1, 2
X_QGA, X_QGR, X_QG1 = 3, 7, 11
Z_KVA, Z_KVAR, Z_KV1, Z_KV1R = 15, 19, 23, 27
X_HX, C_HX, X_STA, X_ST1 = 31, 35, 39, 43
X_GA, X_GHV, X_GHK, X_GHQ = 47, 51, 55, 67
C_DH, H_DH = 59, 61
Y_OA, Y_KA, Y_V1, Y_K1, Y_W1, Y_WA = 62, 63, 64, 65, 66, 83
X_GB, X_GC, X_GD, N_SEM = 71, 75, 79, 86
RING = (1, 2, 3)
CROSS_FIRST = (0,)


def kernel(
    hidden_ref, w_ref, cot_ref, att_ref, dw_ref, dh_ref,
    h_v, w_v, cot_v, far_qg, far_kv, ht, hx, qg, kv, vkt, pt, ut, s_buf, top_buf, st, sm, sm_all, ma, cs, es, rhs,
    ob, ro, kb, rk, ya_s, ya_r, y1_s, y1_r, ywa_s, ywa_r, yw1_s, yw1_r,
    gx_a, gx_h, dwb_a, dwr_a, dwb_h, dwr_h, dhc, dhr,
    sem_l, sem_s, sem_r, sem_os, sem_or, sem_ks, sem_kr, sem_ws, sem_wr,
):
    z, y, x, t = coords()
    other = 1 - y
    core = t % 2
    mate = t + 1 - 2 * core
    across = (t + 2) % 4
    me = lax.axis_index("seq")
    head_a, head_b = 2 * y, 2 - 2 * y

    def at(zz, yy, xx):
        return (seq_of(zz, yy, xx), t)

    def xs(d):
        return (x + d) % NX

    def zs(d):
        return (z + d) % NZ

    def load(i, src, dst):
        return pltpu.make_async_copy(src, dst, sem_l.at[i])

    def load_w(i, c, h):
        cols = aligned(h, HD)
        return load(i, w_ref.at[c, :, cols], w_v.at[c, :, cols])

    local = [load(0, hidden_ref, h_v), load_w(1, 1, head_b), load_w(2, 2, head_b), load_w(3, 1, head_a), load_w(4, 2, head_a)]
    local += [load_w(5, 0, head_b), load_w(6, 0, head_a), load(7, cot_ref, cot_v)]
    local += [load_w(8 + c, c, 1) for c in range(3)]
    for c in local:
        c.start()

    barrier = pltpu.get_barrier_semaphore()
    peers = [at(z, y, xs(d)) for d in RING] + [at(zs(d), y, x) for d in RING]
    peers += [at(z, other, x), (me, mate), (me, across)]
    for peer in peers:
        pl.semaphore_signal(barrier, inc=1, device_id=peer, device_id_type=MESH)
    pl.semaphore_wait(barrier, len(peers))

    def remote(i, src, dst, peer):
        return pltpu.make_async_remote_copy(
            src_ref=src, dst_ref=dst, send_sem=sem_s.at[i], recv_sem=sem_r.at[i],
            device_id=peer, device_id_type=MESH,
        )

    sent = []

    def send(i, src, dst, peer):
        sent.append(remote(i, src, dst, peer))
        sent[-1].start()

    def got(i, dst):
        remote(i, dst, dst, (me, mate)).wait_recv()

    def qg_slot(yy, xx):
        return qg.at[4 + yy * NX + xx]

    def kv_rows(j, yy, zz):
        return kv.at[j, :, aligned(yy * NZ + zz, T), :]

    def columns(c, h):
        return w_v[c, :, aligned(h, HD)]

    def project_kv(h, dst):
        v = dot(h_v[...], jnp.concatenate([columns(1, h), columns(2, h)], axis=1))
        dst[0] = v[:, :HD].astype(BF16)
        dst[1] = v[:, HD:].astype(BF16)

    partner = at(z, other, x)
    own_a, own_1 = qg_slot(y, x), qg.at[x]
    keys_a, keys_1 = kv_rows(1, y, z), kv_rows(0, y, z)
    for c in local[:3]:
        c.wait()
    project_kv(head_b, far_kv)
    send(Y_KVA, far_kv, keys_a, partner)
    for c in local[3:5]:
        c.wait()
    project_kv(head_a, keys_a)
    for d in (1, 3):
        send(Z_KVA + d, keys_a, keys_a, at(zs(d), y, x))
    for c in local[5:8]:
        c.wait()
    own_1[1] = cot_v[:, HD : 2 * HD]
    own_a[1] = cot_v[:, aligned(head_a, HD)]
    far_qg[1] = cot_v[:, aligned(head_b, HD)]
    v = dot(h_v[...], jnp.concatenate([columns(0, head_b), columns(0, head_a)], axis=1))
    far_qg[0] = v[:, :HD].astype(BF16)
    own_a[0] = v[:, HD:].astype(BF16)
    send(Y_QG, far_qg, own_a, partner)
    for d in (1, 3):
        send(X_QGA + d, own_a, own_a, at(z, y, xs(d)))

    got(Y_KVA, kv_rows(1, other, z))
    for d in (1, 3):
        send(Z_KVAR + d, kv_rows(1, other, z), kv_rows(1, other, z), at(zs(d), y, x))

    def forward_keys(base, yy):
        for part, step in ((0, 1), (1, 3)):
            got(base + step, kv_rows(1, yy, zs(4 - step)))
            piece = kv.at[1, part, aligned(yy * NZ + zs(4 - step), T), :]
            send(base + 2 - 2 * part, piece, piece, at(zs(step), y, x))

    def forward_queries(base, yy):
        for part, step in ((0, 1), (1, 3)):
            got(base + step, qg_slot(yy, xs(4 - step)))
            piece = qg.at[4 + yy * NX + xs(4 - step), part]
            send(base + 2 - 2 * part, piece, piece, at(z, y, xs(step)))

    forward_keys(Z_KVA, y)
    for c in local[8:]:
        c.wait()
    project_kv(1, keys_1)
    own_1[0] = dot(h_v[...], columns(0, 1)).astype(BF16)
    got(Y_QG, qg_slot(other, x))
    for d in (1, 3):
        send(X_QGR + d, qg_slot(other, x), qg_slot(other, x), at(z, y, xs(d)))
    forward_queries(X_QGA, y)
    sm[...] = jnp.zeros_like(sm)
    ma[...] = jnp.zeros_like(ma)

    def hidden_rows(i, _):
        ht[i] = h_v[:, aligned(i, 384)].T.reshape(NX, 96, T)
        return 0

    lax.fori_loop(0, NZ * NY, hidden_rows, 0)
    hx[x] = ht[:, x]

    def transpose_block(j, yy, zz):
        i = yy * NZ + zz
        vkt[0:HD, aligned(i, T)] = kv[j, 1, aligned(i, T), :].T
        vkt[HD : 2 * HD, aligned(i, T)] = kv[j, 0, aligned(i, T), :].T

    def transpose_keys(j, base, base_relay):
        def step(d, _):
            zz = zs(4 - d)
            if base is not None:

                @pl.when(d == 2)
                def _():
                    for part in (0, 1):
                        got(base + 2 - 2 * part, kv.at[j, part, aligned(y * NZ + zz, T), :])
                        got(base_relay + 2 - 2 * part, kv.at[j, part, aligned(other * NZ + zz, T), :])

            transpose_block(j, y, zz)
            transpose_block(j, other, zz)
            return 0

        lax.fori_loop(3, 7, lambda d, _: step(d % 4, _), 0)

    forward_keys(Z_KVAR, other)
    forward_queries(X_QGR, other)
    transpose_keys(1, Z_KVA, Z_KVAR)

    send(Y_KV1, keys_1, keys_1, partner)
    half = pl.ds(4 * core, 4)
    rows_sent = []
    for d in (2, 1, 3):
        send(Z_KV1 + d, keys_1, keys_1, at(zs(d), y, x))
        rows_sent.append(remote(X_HX + d, ht.at[half, xs(d)], hx.at[x, half], at(z, y, xs(d))))
        rows_sent[-1].start()
    for d in RING:
        send(X_QG1 + d, own_1, own_1, at(z, y, xs(d)))

    chunks = [slice(c * CHUNK, (c + 1) * CHUNK) for c in range(KEYS // CHUNK)]

    def scores(j, q_slot, c, top):
        s = dot(kv[j, 0, c, :], qg[q_slot, 0], NT)
        s_buf[c] = s
        return jnp.maximum(top, jnp.max(s, axis=0, keepdims=True))

    least = jnp.full((1, T), -jnp.inf, F32)

    def unit(j, q_slot, slot, row, following):
        g = qg[q_slot, 1]
        top = top_buf[0:1] * LOG2
        total, out = 0.0, 0.0
        for c in chunks:
            p = jnp.exp2(s_buf[c] * LOG2 - top)
            total = total + jnp.sum(p, axis=0, keepdims=True)
            p = p.astype(BF16)
            pt[slot, c, :] = p
            out = out + dot(vkt[:, c], p)
        g_t = g.astype(F32).T
        delta = jnp.sum(g_t * out[:HD], axis=0, keepdims=True) / total
        grad, top_next = 0.0, least
        for c in chunks:
            if following is not None:
                top_next = scores(*following, c, top_next)
            dp = dot(kv[j, 1, c, :], g, NT)
            d = (pt[slot, c, :].astype(F32) * (dp - delta)).astype(BF16)
            ut[slot, c, :] = d
            grad = grad + dot(vkt[HD:, c], d)
        st[slot, : 2 * HD] = out
        st[slot, 2 * HD :] = grad
        sm[j, 0, pl.ds(row, 1), :] = top + jnp.log2(total)
        sm[j, 1, pl.ds(row, 1), :] = delta
        ma[j, pl.ds(row, 1), :] = top
        top_buf[0:1] = top_next

    def row_a(i):
        yy = (y + i // 4) % 2
        return yy, xs(4 - i % 4), yy * NX + xs(4 - i % 4)

    def relay_shared():
        rows = kv_rows(0, other, z)
        return [remote(Z_KV1R + d, rows, rows, at(zs(d), y, x)) for d in (1, 3)]

    def cross_shared():
        rows = kv_rows(0, y, zs(2))
        return remote(Z_KV1R + 2, rows, rows, partner)

    def unit_a(i, _):
        _, _, r = row_a(i)
        _, _, r_next = row_a(i + 1)

        @pl.when((i == 1) | (i == 5))
        def _():
            for part in (0, 1):
                got(X_QGA + i + 1 - 2 * part, qg.at[4 + r_next, part])

        @pl.when(i == 3)
        def _():
            got(Y_KV1, kv_rows(0, other, z))
            for c in relay_shared():
                c.start()
            got(Z_KV1 + 2, kv_rows(0, y, zs(2)))
            cross_shared().start()

        @pl.when(i == 7)
        def _():
            for d in (1, 3):
                got(Z_KV1 + d, kv_rows(0, y, zs(4 - d)))
            for d in RING:
                got(Z_KV1R + d, kv_rows(0, other, zs(4 - d)))

        last = i // 7
        unit(1, 4 + r, r, r, (1 - last, jnp.where(last == 1, x, 4 + r_next)))
        return 0

    top = least
    for c in chunks:
        top = scores(1, 4 + y * NX + x, c, top)
    top_buf[0:1] = top
    lax.fori_loop(0, 8, unit_a, 0)
    sent.extend(relay_shared() + [cross_shared()])

    def send_stats(j, base):
        for d in RING:
            send(base + d, sm.at[j], sm_all.at[j, x], at(z, y, xs(d)))
        sm_all[j, x] = sm[j]

    def combine(j, base):
        for d in RING:
            got(base + d, sm_all.at[j, xs(4 - d)])
        lse = sm_all[j, :, 0]
        top = jnp.max(lse, axis=0)
        lse_all = top + jnp.log2(jnp.sum(jnp.exp2(lse - top), axis=0))
        delta = jnp.sum(jnp.exp2(lse - lse_all) * sm_all[j, :, 1], axis=0)
        cs[j] = jnp.exp2(ma[j] - lse_all)
        es[j] = delta - sm[j, 1]

    send_stats(1, X_STA)
    for d in RING:
        part = hx.at[xs(4 - d), half]
        got(X_HX + d, part)
        send(C_HX + d, part, part, (me, mate))
    transpose_keys(0, None, None)
    got(X_QG1 + 1, qg.at[xs(3)])
    unit(0, x, 8, x, (0, xs(3)))
    combine(1, X_STA)

    def prepare(j, row, slot, q_slot, r, b):
        c, e = cs[j, pl.ds(row, 1), :], es[j, pl.ds(row, 1), :]
        o = st[slot, 0:HD] * c
        dq = (st[slot, 2 * HD :] - e * st[slot, HD : 2 * HD]) * (c * SCALE)
        ob[b, 0] = o.T.astype(BF16)
        ob[b, 1] = dq.T.astype(BF16)
        cols = jnp.concatenate([c, e, jnp.zeros((6, T), F32)], axis=0).T
        c, e = cols[:, 0:1], cols[:, 1:2]
        cq = c * qg[q_slot, 0].astype(F32)
        rhs[r, :, 0:HD] = (c * qg[q_slot, 1].astype(F32)).astype(BF16)
        rhs[r, :, HD : 2 * HD] = (e * cq).astype(BF16)
        rhs[r, :, 2 * HD :] = cq.astype(BF16)

    def copy_o(kind, d, b):
        return pltpu.make_async_remote_copy(
            src_ref=ob.at[b], dst_ref=ro.at[kind, x], send_sem=sem_os.at[kind, d], recv_sem=sem_or.at[kind, d],
            device_id=at(z, y, xs(4 - d)), device_id_type=MESH,
        )

    def got_o(kind):
        def step(d):
            dst = ro.at[kind, xs(d)]
            pltpu.make_async_remote_copy(
                src_ref=dst, dst_ref=dst, send_sem=sem_os.at[kind, d], recv_sem=sem_or.at[kind, d],
                device_id=partner, device_id_type=MESH,
            ).wait_recv()

        loop(1, 4, step)

    def send_a(i):
        return copy_o(i // 4, i % 4, row_a(i)[2])

    def loop(first, last, step):
        def body(i, _):
            step(i)
            return 0

        lax.fori_loop(first, last, body, 0)

    def prepare_a(k):
        i = 7 - k
        _, _, r = row_a(i)
        prepare(1, r, r, 4 + r, r, r)

        @pl.when(i % 4 != 0)
        def _():
            send_a(i).start()

    loop(0, 8, prepare_a)
    ro[0, x] = ob[y * NX + x]
    ro[1, x] = ob[other * NX + x]

    def k_block(row, zz):
        return ((y + row) % 2) * NZ + zz

    def k_part(kind):
        return pl.ds(0, 2) if kind < 2 else pl.ds(1, 1) if kind < 4 else pl.ds(0, 1)

    def k_slots(kind):
        return (2 if kind < 2 else 0) + kind % 2

    def copy_k(kind, d):
        src = kb.at[k_block(kind % 2, zs(d)), k_part(kind)]
        return pltpu.make_async_remote_copy(
            src_ref=src, dst_ref=rk.at[k_slots(kind), z, k_part(kind)], send_sem=sem_ks.at[kind, d],
            recv_sem=sem_kr.at[kind, d], device_id=at(zs(d), y, x), device_id_type=MESH,
        )

    def got_k(kind):
        def step(d):
            dst = rk.at[k_slots(kind), zs(4 - d), k_part(kind)]
            pltpu.make_async_remote_copy(
                src_ref=dst, dst_ref=dst, send_sem=sem_ks.at[kind, d],
                recv_sem=sem_kr.at[kind, d], device_id=partner, device_id_type=MESH,
            ).wait_recv()

        loop(1, 4, step)

    def key_blocks(step, kind):
        for row in (1, 0):

            def one(k, row=row):
                zz = 2 * ((z // 2 + 1 + k) % 2)
                b = k_block(row, zz)
                step(b)
                for i in (0, 1):
                    d = (zz + i + NZ - z) % NZ

                    @pl.when(d != 0)
                    def _():
                        copy_k(kind + row, d).start()

            loop(0, 2, one)
            b, part = k_block(row, z), k_part(kind)
            rk[k_slots(kind + row), z, part] = kb[b, part]

    def two_rows(i):
        return pl.ds(pl.multiple_of(i * T, 2 * T), 2 * T)

    def put(b, part, v):
        kb[b, part] = v[:T].astype(BF16)
        kb[b + 1, part] = v[T:].astype(BF16)

    def block_a(i):
        dv = dk = 0.0
        for r in range(8):
            dv = dv + dot(pt[r, two_rows(i), :], rhs[r, :, : 2 * HD])
            dk = dk + dot(ut[r, two_rows(i), :], rhs[r, :, 2 * HD :])
        put(i, 0, (dk - dv[:, HD:]) * SCALE)
        put(i, 1, dv[:, :HD])

    shared_slots = (8, 0, 1, 2)

    def block_v(i):
        dv = 0.0
        for r, slot in enumerate(shared_slots):
            dv = dv + dot(pt[slot, two_rows(i), :], rhs[r, :, : 2 * HD])
        st[i, : 2 * HD, :HD] = dv[:T, HD:]
        st[i + 1, : 2 * HD, :HD] = dv[T:, HD:]
        put(i, 1, dv[:, :HD])

    def block_k(i):
        dk = 0.0
        for r, slot in enumerate(shared_slots):
            dk = dk + dot(ut[slot, two_rows(i), :], rhs[r, :, 2 * HD :])
        put(i, 0, (dk - jnp.concatenate([st[i, : 2 * HD, :HD], st[i + 1, : 2 * HD, :HD]], axis=0)) * SCALE)

    key_blocks(block_a, 0)

    def total(ref, kind, part):
        v = ref[kind, 0, part].astype(F32)
        for i in range(1, 4):
            v = v + ref[kind, i, part].astype(F32)
        return v

    mine, theirs = aligned(y, HD), aligned(other, HD)
    q_part, kv_part = pl.ds(0, 1), pl.ds(1, 2)

    def piece_a(d, part, cols):
        return gx_a.at[xs(d), part, :, cols]

    def gather_a(base, part, cols):
        piece = piece_a(0, part, cols)
        return [remote(base + d, piece, piece, at(z, y, xs(d))) for d in (1, 3)]

    def pass_on(base, part, cols, step):
        piece = piece_a(4 - step, part, cols)
        return remote(base + 2, piece, piece, at(z, y, xs(step)))

    def forward_a(base, part, cols, step):
        got(base + step, piece_a(4 - step, part, cols))
        pass_on(base, part, cols, step).start()

    pieces = {X_GA: (q_part, mine, 1), X_GB: (q_part, theirs, 3), X_GC: (kv_part, mine, 1), X_GD: (kv_part, theirs, 3)}

    def got_a(base):
        part, cols, step = pieces[base]
        got(base + 4 - step, piece_a(step, part, cols))
        got(base + 2, piece_a(2, part, cols))

    def far_o():
        return remote(Y_OA, ya_s.at[pl.ds(0, 2)], ya_r.at[pl.ds(0, 2)], partner)

    def far_k():
        return remote(Y_KA, ya_s.at[pl.ds(2, 2)], ya_r.at[pl.ds(2, 2)], partner)

    def start_all(copies):
        for c in copies:
            c.start()

    def unit_shared(d):
        got(X_QG1 + d + 1, qg.at[xs(3 - d)])
        unit(0, xs(4 - d), d - 1, xs(4 - d), (0, xs(3 - d)))

        @pl.when(d == 1)
        def _():
            got_o(1)
            for part in (0, 1):
                ya_s[part] = total(ro, 1, part).astype(BF16)
            far_o().start()
            got_o(0)
            att_ref[:, aligned(head_a, HD)] = total(ro, 0, 0).astype(BF16)
            gx_a[x, 0, :, mine] = total(ro, 0, 1).astype(BF16)
            start_all(gather_a(X_GA, q_part, mine))

        @pl.when(d == 2)
        def _():
            got_k(1)
            for part in (0, 1):
                ya_s[2 + part] = total(rk, 3, part).astype(BF16)
            far_k().start()
            got(Y_OA, ya_r.at[pl.ds(0, 2)])
            att_ref[:, aligned(head_b, HD)] = ya_r[0]
            gx_a[x, 0, :, theirs] = ya_r[1]
            start_all(gather_a(X_GB, q_part, theirs))
            got_k(0)
            for part in (0, 1):
                gx_a[x, 1 + part, :, mine] = total(rk, 2, part).astype(BF16)
            start_all(gather_a(X_GC, kv_part, mine))
            forward_a(X_GA, q_part, mine, 1)

    loop(1, 3, unit_shared)
    unit(0, xs(1), 2, xs(1), None)
    send_stats(0, X_ST1)
    got(Y_KA, ya_r.at[pl.ds(2, 2)])
    for c in (1, 2):
        gx_a[x, c, :, theirs] = ya_r[1 + c]
    start_all(gather_a(X_GD, kv_part, theirs))
    sent.extend([far_o(), far_k()])
    forward_a(X_GB, q_part, theirs, 3)
    for base, (part, cols, step) in pieces.items():
        sent.extend(gather_a(base, part, cols))
        sent.append(pass_on(base, part, cols, step))

    def copy_w(c, d):
        if c in CROSS_FIRST:
            src, dst = dwb_a.at[zs(d), c, y], dwr_a.at[z, c, y]
        elif c < 3:
            src, dst = dwb_a.at[zs(d), c], dwr_a.at[z, c]
        else:
            src, dst = dwb_h.at[zs(d), c - 3], dwr_h.at[z, c - 3]
        return pltpu.make_async_remote_copy(
            src_ref=src, dst_ref=dst, send_sem=sem_ws.at[c, d],
            recv_sem=sem_wr.at[c, d], device_id=at(zs(d), y, x), device_id_type=MESH,
        )

    def got_w(c):
        def step(d):
            dst = (dwr_h if c >= 3 else dwr_a).at[zs(4 - d), c % 3]
            dst = dst.at[y] if c in CROSS_FIRST else dst
            pltpu.make_async_remote_copy(
                src_ref=dst, dst_ref=dst, send_sem=sem_ws.at[c, d], recv_sem=sem_wr.at[c, d],
                device_id=partner, device_id_type=MESH,
            ).wait_recv()

        loop(1, 4, step)

    def weight_rows(gx, dwb, c):
        def step(i):
            v = 0.0
            for xx in range(NX):
                v = v + dot(hx[xx, pl.ds(i * 4, 4)].reshape(4 * 96, T), gx[xx, c])
            dwb[pl.ds(i * 2, 2), c] = v.astype(BF16).reshape(2, 2, 96, v.shape[1])

        loop(0, 2, step)

    def weight_a(c):
        weight_rows(gx_a, dwb_a, c)
        if c in CROSS_FIRST:
            send(Y_WA + c, dwb_a.at[:, c, other], ywa_r.at[c], partner)
        else:
            loop(1, 4, lambda d: copy_w(c, d).start())
            dwr_a[z, c] = dwb_a[z, c]

    def weight_a_ring(c):
        got(Y_WA + c, ywa_r.at[c])
        dwb_a[:, c, y] = (dwb_a[:, c, y].astype(F32) + ywa_r[c].astype(F32)).astype(BF16)
        loop(1, 4, lambda d: copy_w(c, d).start())
        dwr_a[z, c, y] = dwb_a[z, c, y]

    def weight_shared(c):
        weight_rows(gx_h, dwb_h, c)
        loop(1, 4, lambda d: copy_w(3 + c, d).start())
        dwr_h[z, c] = dwb_h[z, c]

    combine(0, X_ST1)

    def send_shared(d):
        return copy_o(2, d, xs(4 - d))

    def prepare_shared(d):
        slot = (d + 8) % 9
        prepare(0, xs(4 - d), slot, xs(4 - d), d, xs(4 - d))

        @pl.when(d != 0)
        def _():
            send_shared(d).start()

    for c in range(2):
        loop(1, 4, lambda d, c=c: send_a(4 * c + d).wait_send())
    loop(0, 4, prepare_shared)
    ro[2, x] = ob[x]

    forward_a(X_GC, kv_part, mine, 1)
    for kind in (0, 1):
        loop(1, 4, lambda d, kind=kind: copy_k(kind, d).wait_send())
    key_blocks(block_v, 2)
    forward_a(X_GD, kv_part, theirs, 3)
    key_blocks(block_k, 4)

    for d in RING:
        got(C_HX + d, hx.at[xs(4 - d), pl.ds(4 - 4 * core, 4)])
    got_a(X_GA)
    got_a(X_GB)
    weight_a(0)

    got_o(2)
    att_ref[:, HD : 2 * HD] = total(ro, 2, 0).astype(BF16)
    gx_h[x, 0] = total(ro, 2, 1).astype(BF16)

    def gather_shared(base, c):
        for d in RING:
            send(base + d, gx_h.at[x, c], gx_h.at[x, c], at(z, y, xs(d)))

    def got_shared(base, c):
        for d in RING:
            got(base + d, gx_h.at[xs(4 - d), c])

    gather_shared(X_GHQ, 0)
    got_k(3)
    y1_s[1] = total(rk, 1, 1).astype(BF16)
    send(Y_V1, y1_s.at[1], y1_r.at[1], partner)
    weight_a_ring(0)
    got_a(X_GC)
    got_a(X_GD)
    weight_a(2)
    got_k(2)
    got(Y_V1, y1_r.at[1])
    gx_h[x, 2] = (total(rk, 0, 1) + y1_r[1].astype(F32)).astype(BF16)
    gather_shared(X_GHV, 2)
    got_k(5)
    y1_s[0] = total(rk, 1, 0).astype(BF16)
    send(Y_K1, y1_s.at[0], y1_r.at[0], partner)
    weight_a(1)
    got_k(4)
    got(Y_K1, y1_r.at[0])
    gx_h[x, 1] = (total(rk, 0, 0) + y1_r[0].astype(F32)).astype(BF16)
    gather_shared(X_GHK, 1)

    for c in rows_sent:
        c.wait_send()

    def part_of(to):
        return ht.at[pl.ds(2 * to, 2)]

    def hidden_part(to):
        pieces = []
        for i in range(3):
            v = 0.0
            for c in range(3):
                g = jnp.concatenate([gx_a[x, c, :, :HD], gx_h[x, c], gx_a[x, c, :, HD:]], axis=1)
                rows = pl.ds(pl.multiple_of(to * 768 + i * 256, 256), 256)
                v = v + dot(g, w_v[c, rows, :], NT)
            pieces.append(v.astype(BF16))
        part_of(to)[...] = jnp.concatenate(pieces, axis=0).reshape(2, NX, 96, T)

    def copy_mate(i):
        return remote(C_DH + i, part_of(2 * i + 1 - core), dhc.at[i], (me, mate))

    def hidden_pair(i):
        hidden_part(2 * i + 1 - core)
        copy_mate(i).start()
        hidden_part(2 * i + core)

    hi = t // 2
    hidden_pair(1 - hi)
    got(C_DH + 1 - hi, dhc.at[1 - hi])
    far = part_of(across)
    far[...] = (far[...].astype(F32) + dhc[1 - hi].astype(F32)).astype(BF16)
    send(H_DH, far, dhr, (me, across))
    got_shared(X_GHQ, 0)
    weight_shared(0)
    got_shared(X_GHV, 2)
    weight_shared(2)
    got_shared(X_GHK, 1)
    weight_shared(1)
    hidden_pair(hi)
    sent.extend([copy_mate(0), copy_mate(1)])

    def total_w(ref, c, row):
        v = ref[0, c, row].astype(F32)
        for i in range(1, NZ):
            v = v + ref[i, c, row].astype(F32)
        return v

    ring_first = [c for c in range(3) if c not in CROSS_FIRST]
    for c in ring_first:
        got_w(c)
        ywa_s[c] = total_w(dwr_a, c, other).astype(BF16)
        send(Y_WA + c, ywa_s.at[c], ywa_r.at[c, 0], partner)
    for c in range(3):
        got_w(3 + c)
        yw1_s[c] = total_w(dwr_h, c, other).astype(BF16)
    send(Y_W1, yw1_s, yw1_r, partner)
    for c in range(3):
        if c in CROSS_FIRST:
            got_w(c)
        v = total_w(dwr_a, c, y)
        if c in ring_first:
            got(Y_WA + c, ywa_r.at[c, 0])
            v = v + ywa_r[c, 0].astype(F32)
        dw_ref[c, :, :HD] = v[:, :HD]
        dw_ref[c, :, 2 * HD :] = v[:, HD:]
    got(Y_W1, yw1_r)
    for c in range(3):
        dw_ref[c, :, HD : 2 * HD] = total_w(dwr_h, c, y) + yw1_r[c].astype(F32)
    got(C_DH + hi, dhc.at[hi])
    got(H_DH, dhr)
    v = (part_of(t)[...].astype(F32) + dhc[hi].astype(F32) + dhr[...].astype(F32)).astype(BF16).reshape(3 * T, T)
    for i in range(3):
        dh_ref[:, i * T : (i + 1) * T] = v[i * T : (i + 1) * T]

    for c in sent:
        c.wait_send()
    loop(1, 4, lambda d: send_shared(d).wait_send())
    for kind in range(6):
        if kind > 1:
            loop(1, 4, lambda d, kind=kind: copy_k(kind, d).wait_send())
        loop(1, 4, lambda d, c=kind: copy_w(c, d).wait_send())


def call(hidden, weight, cotangent):
    block = (2, T, HD)
    scratch = [
        ((T, 3072), BF16),
        ((3, 3072, 384), BF16),
        ((T, 3 * HD), BF16),
        (block, BF16),
        (block, BF16),
        ((8, NX, 96, T), BF16),
        ((NX, 8, 96, T), BF16),
        ((12,) + block, BF16),
        ((2, 2, KEYS, HD), BF16),
        ((2 * HD, KEYS), BF16),
        ((9, KEYS, T), BF16),
        ((9, KEYS, T), BF16),
        ((KEYS, T), F32),
        ((8, T), F32),
        ((9, 3 * HD, T), F32),
        ((2, 2, 8, T), F32),
        ((2, NX, 2, 8, T), F32),
        ((2, 8, T), F32),
        ((2, 8, T), F32),
        ((2, 8, T), F32),
        ((8, T, 3 * HD), BF16),
        ((8,) + block, BF16),
        ((3, NX) + block, BF16),
        ((8,) + block, BF16),
        ((4, NZ) + block, BF16),
        ((4, T, HD), BF16),
        ((4, T, HD), BF16),
        (block, BF16),
        (block, BF16),
        ((3, 96, 2 * HD), BF16),
        ((3, NZ, 96, 2 * HD), BF16),
        ((3, 96, HD), BF16),
        ((3, 96, HD), BF16),
        ((NX, 3, T, 2 * HD), BF16),
        ((NX, 3, T, HD), BF16),
        ((NZ, 3, 2, 96, 2 * HD), BF16),
        ((NZ, 3, 2, 96, 2 * HD), BF16),
        ((NZ, 3, 2, 96, HD), BF16),
        ((NZ, 3, 2, 96, HD), BF16),
        ((2, 2, NX, 96, T), BF16),
        ((2, NX, 96, T), BF16),
    ]
    sems = [(11,), (N_SEM,), (N_SEM,), (3, 4), (3, 4), (6, 4), (6, 4), (6, 4), (6, 4)]
    vmem = pl.BlockSpec(memory_space=pltpu.VMEM)
    hbm = pl.BlockSpec(memory_space=pl.ANY)
    return pl.pallas_call(
        kernel,
        out_shape=(
            jax.ShapeDtypeStruct((T, 3 * HD), BF16),
            jax.ShapeDtypeStruct((3, 96, 384), F32),
            jax.ShapeDtypeStruct((T, 768), BF16),
        ),
        in_specs=[hbm] * 3,
        out_specs=(vmem,) * 3,
        scratch_shapes=[pltpu.VMEM(*s) for s in scratch] + [pltpu.SemaphoreType.DMA(s) for s in sems],
        compiler_params=pltpu.CompilerParams(
            collective_id=0, has_side_effects=True, vmem_limit_bytes=63 * 2**20
        ),
        cost_estimate=pl.CostEstimate(flops=18 * 10**9, bytes_accessed=10**7, transcendentals=6 * 10**6),
        name="attention_with_gradients",
    )(hidden, weight, cotangent)


def copy_kernel(*refs):
    for src, dst in zip(refs[:3], refs[3:]):
        dst[...] = src[...]


def copy_out(arrays):
    vmem = pl.BlockSpec(memory_space=pltpu.VMEM)
    return pl.pallas_call(
        copy_kernel,
        out_shape=tuple(jax.ShapeDtypeStruct(a.shape, a.dtype) for a in arrays),
        in_specs=[vmem] * 3,
        out_specs=(vmem,) * 3,
        name="copy_out",
    )(*arrays)


def on_device(hidden, qkv_weight, cotangent):
    arrays = call(hidden, qkv_weight.transpose(1, 0, 2), cotangent)
    attention, grad_weight, grad_hidden = copy_out(arrays)
    return attention, grad_hidden, grad_weight.transpose(1, 0, 2)


def solution(mesh):
    in_specs = (P("seq", None), P(None, None, "tp"), P("seq", "tp"))
    out_specs = (P("seq", "tp"), P("seq", "tp"), P("seq", None, "tp"))
    return jax.shard_map(
        on_device, mesh=mesh, in_specs=in_specs, out_specs=out_specs, check_vma=False
    )
```

```python
import math

import jax
import jax.numpy as jnp
from jax import lax
from jax.experimental import pallas as pl
from jax.experimental.pallas import tpu as pltpu
from jax.sharding import PartitionSpec as P

HD = 128
T = 256
NZ, NY, NX = 4, 2, 4
KEYS = NZ * NY * T
CHUNK = 512
SCALE = 1.0 / math.sqrt(HD)
LOG2 = SCALE * math.log2(math.e)
MESH = pl.DeviceIdType.MESH
F32, BF16 = jnp.float32, jnp.bfloat16
NN = (((1,), (0,)), ((), ()))
NT = (((1,), (1,)), ((), ()))


def dot(a, b, dims=NN):
    return lax.dot_general(a, b, dims, preferred_element_type=F32)


def coords():
    s = lax.axis_index("seq")
    return s // (NY * NX), (s // NX) % NY, s % NX, lax.axis_index("tp")


def seq_of(z, y, x):
    return (z * NY + y) * NX + x


def aligned(i, n):
    return pl.ds(pl.multiple_of(i * n, n), n)

Y_QG, Y_KVA, Y_KV1 = 0, 1, 2
X_QGA, X_QGR, X_QG1 = 3, 7, 11
Z_KVA, Z_KVAR, Z_KV1, Z_KV1R = 15, 19, 23, 27
X_HX, C_HX, X_STA, X_ST1 = 31, 35, 39, 43
X_GA, X_GHV, X_GHK, X_GHQ = 47, 51, 55, 67
C_DH, H_DH = 59, 61
Y_OA, Y_KA, Y_V1, Y_K1, Y_W1, Y_WA = 62, 63, 64, 65, 66, 83
X_GB, X_GC, X_GD, N_SEM = 71, 75, 79, 86
RING = (1, 2, 3)
CROSS_FIRST = (0,)


def kernel(
    hidden_ref, w_ref, cot_ref, att_ref, dw_ref, dh_ref,
    h_v, w_v, cot_v, far_qg, far_kv, ht, hx, qg, kv, vkt, pt, ut, s_buf, top_buf, st, sm, sm_all, ma, cs, es, rhs,
    ob, ro, kb, rk, ya_s, ya_r, y1_s, y1_r, ywa_s, ywa_r, yw1_s, yw1_r,
    gx_a, gx_h, dwb_a, dwr_a, dwb_h, dwr_h, dhc, dhr,
    sem_l, sem_s, sem_r, sem_os, sem_or, sem_ks, sem_kr, sem_ws, sem_wr,
):
    z, y, x, t = coords()
    other = 1 - y
    core = t % 2
    mate = t + 1 - 2 * core
    across = (t + 2) % 4
    me = lax.axis_index("seq")
    head_a, head_b = 2 * y, 2 - 2 * y

    def at(zz, yy, xx):
        return (seq_of(zz, yy, xx), t)

    def xs(d):
        return (x + d) % NX

    def zs(d):
        return (z + d) % NZ

    def load(i, src, dst):
        return pltpu.make_async_copy(src, dst, sem_l.at[i])

    def load_w(i, c, h):
        cols = aligned(h, HD)
        return load(i, w_ref.at[c, :, cols], w_v.at[c, :, cols])

    local = [load(0, hidden_ref, h_v), load_w(1, 1, head_b), load_w(2, 2, head_b), load_w(3, 1, head_a), load_w(4, 2, head_a)]
    local += [load_w(5, 0, head_b), load_w(6, 0, head_a), load(7, cot_ref, cot_v)]
    local += [load_w(8 + c, c, 1) for c in range(3)]
    for c in local:
        c.start()

    barrier = pltpu.get_barrier_semaphore()
    peers = [at(z, y, xs(d)) for d in RING] + [at(zs(d), y, x) for d in RING]
    peers += [at(z, other, x), (me, mate), (me, across)]
    for peer in peers:
        pl.semaphore_signal(barrier, inc=1, device_id=peer, device_id_type=MESH)
    pl.semaphore_wait(barrier, len(peers))

    def remote(i, src, dst, peer):
        return pltpu.make_async_remote_copy(
            src_ref=src, dst_ref=dst, send_sem=sem_s.at[i], recv_sem=sem_r.at[i],
            device_id=peer, device_id_type=MESH,
        )

    sent = []

    def send(i, src, dst, peer):
        sent.append(remote(i, src, dst, peer))
        sent[-1].start()

    def got(i, dst):
        remote(i, dst, dst, (me, mate)).wait_recv()

    def qg_slot(yy, xx):
        return qg.at[4 + yy * NX + xx]

    def kv_rows(j, yy, zz):
        return kv.at[j, :, aligned(yy * NZ + zz, T), :]

    def columns(c, h):
        return w_v[c, :, aligned(h, HD)]

    def project_kv(h, dst):
        v = dot(h_v[...], jnp.concatenate([columns(1, h), columns(2, h)], axis=1))
        dst[0] = v[:, :HD].astype(BF16)
        dst[1] = v[:, HD:].astype(BF16)

    partner = at(z, other, x)
    own_a, own_1 = qg_slot(y, x), qg.at[x]
    keys_a, keys_1 = kv_rows(1, y, z), kv_rows(0, y, z)
    for c in local[:3]:
        c.wait()
    project_kv(head_b, far_kv)
    send(Y_KVA, far_kv, keys_a, partner)
    for c in local[3:5]:
        c.wait()
    project_kv(head_a, keys_a)
    for d in (1, 3):
        send(Z_KVA + d, keys_a, keys_a, at(zs(d), y, x))
    for c in local[5:8]:
        c.wait()
    own_1[1] = cot_v[:, HD : 2 * HD]
    own_a[1] = cot_v[:, aligned(head_a, HD)]
    far_qg[1] = cot_v[:, aligned(head_b, HD)]
    v = dot(h_v[...], jnp.concatenate([columns(0, head_b), columns(0, head_a)], axis=1))
    far_qg[0] = v[:, :HD].astype(BF16)
    own_a[0] = v[:, HD:].astype(BF16)
    send(Y_QG, far_qg, own_a, partner)
    for d in (1, 3):
        send(X_QGA + d, own_a, own_a, at(z, y, xs(d)))

    got(Y_KVA, kv_rows(1, other, z))
    for d in (1, 3):
        send(Z_KVAR + d, kv_rows(1, other, z), kv_rows(1, other, z), at(zs(d), y, x))

    def forward_keys(base, yy):
        for part, step in ((0, 1), (1, 3)):
            got(base + step, kv_rows(1, yy, zs(4 - step)))
            piece = kv.at[1, part, aligned(yy * NZ + zs(4 - step), T), :]
            send(base + 2 - 2 * part, piece, piece, at(zs(step), y, x))

    def forward_queries(base, yy):
        for part, step in ((0, 1), (1, 3)):
            got(base + step, qg_slot(yy, xs(4 - step)))
            piece = qg.at[4 + yy * NX + xs(4 - step), part]
            send(base + 2 - 2 * part, piece, piece, at(z, y, xs(step)))

    forward_keys(Z_KVA, y)
    for c in local[8:]:
        c.wait()
    project_kv(1, keys_1)
    own_1[0] = dot(h_v[...], columns(0, 1)).astype(BF16)
    got(Y_QG, qg_slot(other, x))
    for d in (1, 3):
        send(X_QGR + d, qg_slot(other, x), qg_slot(other, x), at(z, y, xs(d)))
    forward_queries(X_QGA, y)
    sm[...] = jnp.zeros_like(sm)
    ma[...] = jnp.zeros_like(ma)

    def hidden_rows(i, _):
        ht[i] = h_v[:, aligned(i, 384)].T.reshape(NX, 96, T)
        return 0

    lax.fori_loop(0, NZ * NY, hidden_rows, 0)
    hx[x] = ht[:, x]

    def transpose_block(j, yy, zz):
        i = yy * NZ + zz
        vkt[0:HD, aligned(i, T)] = kv[j, 1, aligned(i, T), :].T
        vkt[HD : 2 * HD, aligned(i, T)] = kv[j, 0, aligned(i, T), :].T

    def transpose_keys(j, base, base_relay):
        def step(d, _):
            zz = zs(4 - d)
            if base is not None:

                @pl.when(d == 2)
                def _():
                    for part in (0, 1):
                        got(base + 2 - 2 * part, kv.at[j, part, aligned(y * NZ + zz, T), :])
                        got(base_relay + 2 - 2 * part, kv.at[j, part, aligned(other * NZ + zz, T), :])

            transpose_block(j, y, zz)
            transpose_block(j, other, zz)
            return 0

        lax.fori_loop(3, 7, lambda d, _: step(d % 4, _), 0)

    forward_keys(Z_KVAR, other)
    forward_queries(X_QGR, other)
    transpose_keys(1, Z_KVA, Z_KVAR)

    send(Y_KV1, keys_1, keys_1, partner)
    half = pl.ds(4 * core, 4)
    rows_sent = []
    for d in (2, 1, 3):
        send(Z_KV1 + d, keys_1, keys_1, at(zs(d), y, x))
        rows_sent.append(remote(X_HX + d, ht.at[half, xs(d)], hx.at[x, half], at(z, y, xs(d))))
        rows_sent[-1].start()
    for d in RING:
        send(X_QG1 + d, own_1, own_1, at(z, y, xs(d)))

    chunks = [slice(c * CHUNK, (c + 1) * CHUNK) for c in range(KEYS // CHUNK)]

    def scores(j, q_slot, c, top):
        s = dot(kv[j, 0, c, :], qg[q_slot, 0], NT)
        s_buf[c] = s
        return jnp.maximum(top, jnp.max(s, axis=0, keepdims=True))

    least = jnp.full((1, T), -jnp.inf, F32)

    def unit(j, q_slot, slot, row, following):
        g = qg[q_slot, 1]
        top = top_buf[0:1] * LOG2
        total, out = 0.0, 0.0
        for c in chunks:
            p = jnp.exp2(s_buf[c] * LOG2 - top)
            total = total + jnp.sum(p, axis=0, keepdims=True)
            p = p.astype(BF16)
            pt[slot, c, :] = p
            out = out + dot(vkt[:, c], p)
        g_t = g.astype(F32).T
        delta = jnp.sum(g_t * out[:HD], axis=0, keepdims=True) / total
        grad, top_next = 0.0, least
        for c in chunks:
            if following is not None:
                top_next = scores(*following, c, top_next)
            dp = dot(kv[j, 1, c, :], g, NT)
            d = (pt[slot, c, :].astype(F32) * (dp - delta)).astype(BF16)
            ut[slot, c, :] = d
            grad = grad + dot(vkt[HD:, c], d)
        st[slot, : 2 * HD] = out
        st[slot, 2 * HD :] = grad
        sm[j, 0, pl.ds(row, 1), :] = top + jnp.log2(total)
        sm[j, 1, pl.ds(row, 1), :] = delta
        ma[j, pl.ds(row, 1), :] = top
        top_buf[0:1] = top_next

    def row_a(i):
        yy = (y + i // 4) % 2
        return yy, xs(4 - i % 4), yy * NX + xs(4 - i % 4)

    def relay_shared():
        rows = kv_rows(0, other, z)
        return [remote(Z_KV1R + d, rows, rows, at(zs(d), y, x)) for d in (1, 3)]

    def cross_shared():
        rows = kv_rows(0, y, zs(2))
        return remote(Z_KV1R + 2, rows, rows, partner)

    def unit_a(i, _):
        _, _, r = row_a(i)
        _, _, r_next = row_a(i + 1)

        @pl.when((i == 1) | (i == 5))
        def _():
            for part in (0, 1):
                got(X_QGA + i + 1 - 2 * part, qg.at[4 + r_next, part])

        @pl.when(i == 3)
        def _():
            got(Y_KV1, kv_rows(0, other, z))
            for c in relay_shared():
                c.start()
            got(Z_KV1 + 2, kv_rows(0, y, zs(2)))
            cross_shared().start()

        @pl.when(i == 7)
        def _():
            for d in (1, 3):
                got(Z_KV1 + d, kv_rows(0, y, zs(4 - d)))
            for d in RING:
                got(Z_KV1R + d, kv_rows(0, other, zs(4 - d)))

        last = i // 7
        unit(1, 4 + r, r, r, (1 - last, jnp.where(last == 1, x, 4 + r_next)))
        return 0

    top = least
    for c in chunks:
        top = scores(1, 4 + y * NX + x, c, top)
    top_buf[0:1] = top
    lax.fori_loop(0, 8, unit_a, 0)
    sent.extend(relay_shared() + [cross_shared()])

    def send_stats(j, base):
        for d in RING:
            send(base + d, sm.at[j], sm_all.at[j, x], at(z, y, xs(d)))
        sm_all[j, x] = sm[j]

    def combine(j, base):
        for d in RING:
            got(base + d, sm_all.at[j, xs(4 - d)])
        lse = sm_all[j, :, 0]
        top = jnp.max(lse, axis=0)
        lse_all = top + jnp.log2(jnp.sum(jnp.exp2(lse - top), axis=0))
        delta = jnp.sum(jnp.exp2(lse - lse_all) * sm_all[j, :, 1], axis=0)
        cs[j] = jnp.exp2(ma[j] - lse_all)
        es[j] = delta - sm[j, 1]

    send_stats(1, X_STA)
    for d in RING:
        part = hx.at[xs(4 - d), half]
        got(X_HX + d, part)
        send(C_HX + d, part, part, (me, mate))
    transpose_keys(0, None, None)
    got(X_QG1 + 1, qg.at[xs(3)])
    unit(0, x, 8, x, (0, xs(3)))
    combine(1, X_STA)

    def prepare(j, row, slot, q_slot, r, b):
        c, e = cs[j, pl.ds(row, 1), :], es[j, pl.ds(row, 1), :]
        o = st[slot, 0:HD] * c
        dq = (st[slot, 2 * HD :] - e * st[slot, HD : 2 * HD]) * (c * SCALE)
        ob[b, 0] = o.T.astype(BF16)
        ob[b, 1] = dq.T.astype(BF16)
        cols = jnp.concatenate([c, e, jnp.zeros((6, T), F32)], axis=0).T
        c, e = cols[:, 0:1], cols[:, 1:2]
        cq = c * qg[q_slot, 0].astype(F32)
        rhs[r, :, 0:HD] = (c * qg[q_slot, 1].astype(F32)).astype(BF16)
        rhs[r, :, HD : 2 * HD] = (e * cq).astype(BF16)
        rhs[r, :, 2 * HD :] = cq.astype(BF16)

    def copy_o(kind, d, b):
        return pltpu.make_async_remote_copy(
            src_ref=ob.at[b], dst_ref=ro.at[kind, x], send_sem=sem_os.at[kind, d], recv_sem=sem_or.at[kind, d],
            device_id=at(z, y, xs(4 - d)), device_id_type=MESH,
        )

    def got_o(kind):
        def step(d):
            dst = ro.at[kind, xs(d)]
            pltpu.make_async_remote_copy(
                src_ref=dst, dst_ref=dst, send_sem=sem_os.at[kind, d], recv_sem=sem_or.at[kind, d],
                device_id=partner, device_id_type=MESH,
            ).wait_recv()

        loop(1, 4, step)

    def send_a(i):
        return copy_o(i // 4, i % 4, row_a(i)[2])

    def loop(first, last, step):
        def body(i, _):
            step(i)
            return 0

        lax.fori_loop(first, last, body, 0)

    def prepare_a(k):
        i = 7 - k
        _, _, r = row_a(i)
        prepare(1, r, r, 4 + r, r, r)

        @pl.when(i % 4 != 0)
        def _():
            send_a(i).start()

    loop(0, 8, prepare_a)
    ro[0, x] = ob[y * NX + x]
    ro[1, x] = ob[other * NX + x]

    def k_block(row, zz):
        return ((y + row) % 2) * NZ + zz

    def k_part(kind):
        return pl.ds(0, 2) if kind < 2 else pl.ds(1, 1) if kind < 4 else pl.ds(0, 1)

    def k_slots(kind):
        return (2 if kind < 2 else 0) + kind % 2

    def copy_k(kind, d):
        src = kb.at[k_block(kind % 2, zs(d)), k_part(kind)]
        return pltpu.make_async_remote_copy(
            src_ref=src, dst_ref=rk.at[k_slots(kind), z, k_part(kind)], send_sem=sem_ks.at[kind, d],
            recv_sem=sem_kr.at[kind, d], device_id=at(zs(d), y, x), device_id_type=MESH,
        )

    def got_k(kind):
        def step(d):
            dst = rk.at[k_slots(kind), zs(4 - d), k_part(kind)]
            pltpu.make_async_remote_copy(
                src_ref=dst, dst_ref=dst, send_sem=sem_ks.at[kind, d],
                recv_sem=sem_kr.at[kind, d], device_id=partner, device_id_type=MESH,
            ).wait_recv()

        loop(1, 4, step)

    def key_blocks(step, kind):
        for row in (1, 0):

            def one(k, row=row):
                zz = 2 * ((z // 2 + 1 + k) % 2)
                b = k_block(row, zz)
                step(b)
                for i in (0, 1):
                    d = (zz + i + NZ - z) % NZ

                    @pl.when(d != 0)
                    def _():
                        copy_k(kind + row, d).start()

            loop(0, 2, one)
            b, part = k_block(row, z), k_part(kind)
            rk[k_slots(kind + row), z, part] = kb[b, part]

    def two_rows(i):
        return pl.ds(pl.multiple_of(i * T, 2 * T), 2 * T)

    def put(b, part, v):
        kb[b, part] = v[:T].astype(BF16)
        kb[b + 1, part] = v[T:].astype(BF16)

    def block_a(i):
        dv = dk = 0.0
        for r in range(8):
            dv = dv + dot(pt[r, two_rows(i), :], rhs[r, :, : 2 * HD])
            dk = dk + dot(ut[r, two_rows(i), :], rhs[r, :, 2 * HD :])
        put(i, 0, (dk - dv[:, HD:]) * SCALE)
        put(i, 1, dv[:, :HD])

    shared_slots = (8, 0, 1, 2)

    def block_v(i):
        dv = 0.0
        for r, slot in enumerate(shared_slots):
            dv = dv + dot(pt[slot, two_rows(i), :], rhs[r, :, : 2 * HD])
        st[i, : 2 * HD, :HD] = dv[:T, HD:]
        st[i + 1, : 2 * HD, :HD] = dv[T:, HD:]
        put(i, 1, dv[:, :HD])

    def block_k(i):
        dk = 0.0
        for r, slot in enumerate(shared_slots):
            dk = dk + dot(ut[slot, two_rows(i), :], rhs[r, :, 2 * HD :])
        put(i, 0, (dk - jnp.concatenate([st[i, : 2 * HD, :HD], st[i + 1, : 2 * HD, :HD]], axis=0)) * SCALE)

    key_blocks(block_a, 0)

    def total(ref, kind, part):
        v = ref[kind, 0, part].astype(F32)
        for i in range(1, 4):
            v = v + ref[kind, i, part].astype(F32)
        return v

    mine, theirs = aligned(y, HD), aligned(other, HD)
    q_part, kv_part = pl.ds(0, 1), pl.ds(1, 2)

    def piece_a(d, part, cols):
        return gx_a.at[xs(d), part, :, cols]

    def gather_a(base, part, cols):
        piece = piece_a(0, part, cols)
        return [remote(base + d, piece, piece, at(z, y, xs(d))) for d in (1, 3)]

    def pass_on(base, part, cols, step):
        piece = piece_a(4 - step, part, cols)
        return remote(base + 2, piece, piece, at(z, y, xs(step)))

    def forward_a(base, part, cols, step):
        got(base + step, piece_a(4 - step, part, cols))
        pass_on(base, part, cols, step).start()

    pieces = {X_GA: (q_part, mine, 1), X_GB: (q_part, theirs, 3), X_GC: (kv_part, mine, 1), X_GD: (kv_part, theirs, 3)}

    def got_a(base):
        part, cols, step = pieces[base]
        got(base + 4 - step, piece_a(step, part, cols))
        got(base + 2, piece_a(2, part, cols))

    def far_o():
        return remote(Y_OA, ya_s.at[pl.ds(0, 2)], ya_r.at[pl.ds(0, 2)], partner)

    def far_k():
        return remote(Y_KA, ya_s.at[pl.ds(2, 2)], ya_r.at[pl.ds(2, 2)], partner)

    def start_all(copies):
        for c in copies:
            c.start()

    def unit_shared(d):
        got(X_QG1 + d + 1, qg.at[xs(3 - d)])
        unit(0, xs(4 - d), d - 1, xs(4 - d), (0, xs(3 - d)))

        @pl.when(d == 1)
        def _():
            got_o(1)
            for part in (0, 1):
                ya_s[part] = total(ro, 1, part).astype(BF16)
            far_o().start()
            got_o(0)
            att_ref[:, aligned(head_a, HD)] = total(ro, 0, 0).astype(BF16)
            gx_a[x, 0, :, mine] = total(ro, 0, 1).astype(BF16)
            start_all(gather_a(X_GA, q_part, mine))

        @pl.when(d == 2)
        def _():
            got_k(1)
            for part in (0, 1):
                ya_s[2 + part] = total(rk, 3, part).astype(BF16)
            far_k().start()
            got(Y_OA, ya_r.at[pl.ds(0, 2)])
            att_ref[:, aligned(head_b, HD)] = ya_r[0]
            gx_a[x, 0, :, theirs] = ya_r[1]
            start_all(gather_a(X_GB, q_part, theirs))
            got_k(0)
            for part in (0, 1):
                gx_a[x, 1 + part, :, mine] = total(rk, 2, part).astype(BF16)
            start_all(gather_a(X_GC, kv_part, mine))
            forward_a(X_GA, q_part, mine, 1)

    loop(1, 3, unit_shared)
    unit(0, xs(1), 2, xs(1), None)
    send_stats(0, X_ST1)
    got(Y_KA, ya_r.at[pl.ds(2, 2)])
    for c in (1, 2):
        gx_a[x, c, :, theirs] = ya_r[1 + c]
    start_all(gather_a(X_GD, kv_part, theirs))
    sent.extend([far_o(), far_k()])
    forward_a(X_GB, q_part, theirs, 3)
    for base, (part, cols, step) in pieces.items():
        sent.extend(gather_a(base, part, cols))
        sent.append(pass_on(base, part, cols, step))

    def copy_w(c, d):
        if c in CROSS_FIRST:
            src, dst = dwb_a.at[zs(d), c, y], dwr_a.at[z, c, y]
        elif c < 3:
            src, dst = dwb_a.at[zs(d), c], dwr_a.at[z, c]
        else:
            src, dst = dwb_h.at[zs(d), c - 3], dwr_h.at[z, c - 3]
        return pltpu.make_async_remote_copy(
            src_ref=src, dst_ref=dst, send_sem=sem_ws.at[c, d],
            recv_sem=sem_wr.at[c, d], device_id=at(zs(d), y, x), device_id_type=MESH,
        )

    def got_w(c):
        def step(d):
            dst = (dwr_h if c >= 3 else dwr_a).at[zs(4 - d), c % 3]
            dst = dst.at[y] if c in CROSS_FIRST else dst
            pltpu.make_async_remote_copy(
                src_ref=dst, dst_ref=dst, send_sem=sem_ws.at[c, d], recv_sem=sem_wr.at[c, d],
                device_id=partner, device_id_type=MESH,
            ).wait_recv()

        loop(1, 4, step)

    def weight_rows(gx, dwb, c):
        def step(i):
            v = 0.0
            for xx in range(NX):
                v = v + dot(hx[xx, pl.ds(i * 4, 4)].reshape(4 * 96, T), gx[xx, c])
            dwb[pl.ds(i * 2, 2), c] = v.astype(BF16).reshape(2, 2, 96, v.shape[1])

        loop(0, 2, step)

    def weight_a(c):
        weight_rows(gx_a, dwb_a, c)
        if c in CROSS_FIRST:
            send(Y_WA + c, dwb_a.at[:, c, other], ywa_r.at[c], partner)
        else:
            loop(1, 4, lambda d: copy_w(c, d).start())
            dwr_a[z, c] = dwb_a[z, c]

    def weight_a_ring(c):
        got(Y_WA + c, ywa_r.at[c])
        dwb_a[:, c, y] = (dwb_a[:, c, y].astype(F32) + ywa_r[c].astype(F32)).astype(BF16)
        loop(1, 4, lambda d: copy_w(c, d).start())
        dwr_a[z, c, y] = dwb_a[z, c, y]

    def weight_shared(c):
        weight_rows(gx_h, dwb_h, c)
        loop(1, 4, lambda d: copy_w(3 + c, d).start())
        dwr_h[z, c] = dwb_h[z, c]

    for c in rows_sent:
        c.wait_send()

    def part_of(to):
        return ht.at[pl.ds(2 * to, 2)]

    def hidden_sum(to, term):
        pieces = []
        for i in range(3):
            rows = pl.ds(pl.multiple_of(to * 768 + i * 256, 256), 256)
            pieces.append(term(0, rows) + term(1, rows) + term(2, rows))
        return jnp.concatenate(pieces, axis=0)

    def term_a(c, rows):
        w = jnp.concatenate([w_v[c, rows, :HD], w_v[c, rows, 2 * HD :]], axis=1)
        return dot(gx_a[x, c], w, NT)

    def term_shared(c, rows):
        return dot(gx_h[x, c], w_v[c, rows, HD : 2 * HD], NT)

    def hidden_first(to):
        part_of(to)[...] = hidden_sum(to, term_a).astype(BF16).reshape(2, NX, 96, T)

    def hidden_part(to):
        v = part_of(to)[...].astype(F32).reshape(3 * T, T) + hidden_sum(to, term_shared)
        part_of(to)[...] = v.astype(BF16).reshape(2, NX, 96, T)

    loop(0, 4, hidden_first)
    combine(0, X_ST1)

    def send_shared(d):
        return copy_o(2, d, xs(4 - d))

    def prepare_shared(d):
        slot = (d + 8) % 9
        prepare(0, xs(4 - d), slot, xs(4 - d), d, xs(4 - d))

        @pl.when(d != 0)
        def _():
            send_shared(d).start()

    for c in range(2):
        loop(1, 4, lambda d, c=c: send_a(4 * c + d).wait_send())
    loop(0, 4, prepare_shared)
    ro[2, x] = ob[x]

    for kind in (0, 1):
        loop(1, 4, lambda d, kind=kind: copy_k(kind, d).wait_send())
    key_blocks(block_v, 2)
    forward_a(X_GC, kv_part, mine, 1)
    forward_a(X_GD, kv_part, theirs, 3)
    for d in RING:
        got(C_HX + d, hx.at[xs(4 - d), pl.ds(4 - 4 * core, 4)])
    got_a(X_GA)
    got_a(X_GB)
    weight_a(0)
    key_blocks(block_k, 4)


    got_o(2)
    att_ref[:, HD : 2 * HD] = total(ro, 2, 0).astype(BF16)
    gx_h[x, 0] = total(ro, 2, 1).astype(BF16)

    def gather_shared(base, c):
        for d in RING:
            send(base + d, gx_h.at[x, c], gx_h.at[x, c], at(z, y, xs(d)))

    def got_shared(base, c):
        for d in RING:
            got(base + d, gx_h.at[xs(4 - d), c])

    gather_shared(X_GHQ, 0)
    got_k(3)
    y1_s[1] = total(rk, 1, 1).astype(BF16)
    send(Y_V1, y1_s.at[1], y1_r.at[1], partner)
    weight_a_ring(0)
    got_a(X_GC)
    got_a(X_GD)
    weight_a(2)
    got_k(2)
    got(Y_V1, y1_r.at[1])
    gx_h[x, 2] = (total(rk, 0, 1) + y1_r[1].astype(F32)).astype(BF16)
    gather_shared(X_GHV, 2)
    got_k(5)
    y1_s[0] = total(rk, 1, 0).astype(BF16)
    send(Y_K1, y1_s.at[0], y1_r.at[0], partner)
    weight_a(1)
    got_k(4)
    got(Y_K1, y1_r.at[0])
    gx_h[x, 1] = (total(rk, 0, 0) + y1_r[0].astype(F32)).astype(BF16)
    gather_shared(X_GHK, 1)

    def copy_mate(i):
        return remote(C_DH + i, part_of(2 * i + 1 - core), dhc.at[i], (me, mate))

    def hidden_pair(i):
        hidden_part(2 * i + 1 - core)
        copy_mate(i).start()
        hidden_part(2 * i + core)

    hi = t // 2
    hidden_pair(1 - hi)
    got(C_DH + 1 - hi, dhc.at[1 - hi])
    far = part_of(across)
    far[...] = (far[...].astype(F32) + dhc[1 - hi].astype(F32)).astype(BF16)
    send(H_DH, far, dhr, (me, across))
    got_shared(X_GHQ, 0)
    weight_shared(0)
    got_shared(X_GHV, 2)
    weight_shared(2)
    got_shared(X_GHK, 1)
    weight_shared(1)
    hidden_pair(hi)
    sent.extend([copy_mate(0), copy_mate(1)])

    def total_w(ref, c, row):
        v = ref[0, c, row].astype(F32)
        for i in range(1, NZ):
            v = v + ref[i, c, row].astype(F32)
        return v

    ring_first = [c for c in range(3) if c not in CROSS_FIRST]
    for c in ring_first:
        got_w(c)
        ywa_s[c] = total_w(dwr_a, c, other).astype(BF16)
        send(Y_WA + c, ywa_s.at[c], ywa_r.at[c, 0], partner)
    for c in range(3):
        got_w(3 + c)
        yw1_s[c] = total_w(dwr_h, c, other).astype(BF16)
    send(Y_W1, yw1_s, yw1_r, partner)
    for c in range(3):
        if c in CROSS_FIRST:
            got_w(c)
        v = total_w(dwr_a, c, y)
        if c in ring_first:
            got(Y_WA + c, ywa_r.at[c, 0])
            v = v + ywa_r[c, 0].astype(F32)
        dw_ref[c, :, :HD] = v[:, :HD]
        dw_ref[c, :, 2 * HD :] = v[:, HD:]
    got(Y_W1, yw1_r)
    for c in range(3):
        dw_ref[c, :, HD : 2 * HD] = total_w(dwr_h, c, y) + yw1_r[c].astype(F32)
    got(C_DH + hi, dhc.at[hi])
    got(H_DH, dhr)
    v = (part_of(t)[...].astype(F32) + dhc[hi].astype(F32) + dhr[...].astype(F32)).astype(BF16).reshape(3 * T, T)
    for i in range(3):
        dh_ref[:, i * T : (i + 1) * T] = v[i * T : (i + 1) * T]

    for c in sent:
        c.wait_send()
    loop(1, 4, lambda d: send_shared(d).wait_send())
    for kind in range(6):
        if kind > 1:
            loop(1, 4, lambda d, kind=kind: copy_k(kind, d).wait_send())
        loop(1, 4, lambda d, c=kind: copy_w(c, d).wait_send())


def call(hidden, weight, cotangent):
    block = (2, T, HD)
    scratch = [
        ((T, 3072), BF16),
        ((3, 3072, 384), BF16),
        ((T, 3 * HD), BF16),
        (block, BF16),
        (block, BF16),
        ((8, NX, 96, T), BF16),
        ((NX, 8, 96, T), BF16),
        ((12,) + block, BF16),
        ((2, 2, KEYS, HD), BF16),
        ((2 * HD, KEYS), BF16),
        ((9, KEYS, T), BF16),
        ((9, KEYS, T), BF16),
        ((KEYS, T), F32),
        ((8, T), F32),
        ((9, 3 * HD, T), F32),
        ((2, 2, 8, T), F32),
        ((2, NX, 2, 8, T), F32),
        ((2, 8, T), F32),
        ((2, 8, T), F32),
        ((2, 8, T), F32),
        ((8, T, 3 * HD), BF16),
        ((8,) + block, BF16),
        ((3, NX) + block, BF16),
        ((8,) + block, BF16),
        ((4, NZ) + block, BF16),
        ((4, T, HD), BF16),
        ((4, T, HD), BF16),
        (block, BF16),
        (block, BF16),
        ((3, 96, 2 * HD), BF16),
        ((3, NZ, 96, 2 * HD), BF16),
        ((3, 96, HD), BF16),
        ((3, 96, HD), BF16),
        ((NX, 3, T, 2 * HD), BF16),
        ((NX, 3, T, HD), BF16),
        ((NZ, 3, 2, 96, 2 * HD), BF16),
        ((NZ, 3, 2, 96, 2 * HD), BF16),
        ((NZ, 3, 2, 96, HD), BF16),
        ((NZ, 3, 2, 96, HD), BF16),
        ((2, 2, NX, 96, T), BF16),
        ((2, NX, 96, T), BF16),
    ]
    sems = [(11,), (N_SEM,), (N_SEM,), (3, 4), (3, 4), (6, 4), (6, 4), (6, 4), (6, 4)]
    vmem = pl.BlockSpec(memory_space=pltpu.VMEM)
    hbm = pl.BlockSpec(memory_space=pl.ANY)
    return pl.pallas_call(
        kernel,
        out_shape=(
            jax.ShapeDtypeStruct((T, 3 * HD), BF16),
            jax.ShapeDtypeStruct((3, 96, 384), F32),
            jax.ShapeDtypeStruct((T, 768), BF16),
        ),
        in_specs=[hbm] * 3,
        out_specs=(vmem,) * 3,
        scratch_shapes=[pltpu.VMEM(*s) for s in scratch] + [pltpu.SemaphoreType.DMA(s) for s in sems],
        compiler_params=pltpu.CompilerParams(
            collective_id=0, has_side_effects=True, vmem_limit_bytes=63 * 2**20
        ),
        cost_estimate=pl.CostEstimate(flops=18 * 10**9, bytes_accessed=10**7, transcendentals=6 * 10**6),
        name="attention_with_gradients",
    )(hidden, weight, cotangent)


def copy_kernel(*refs):
    for src, dst in zip(refs[:3], refs[3:]):
        dst[...] = src[...]


def copy_out(arrays):
    vmem = pl.BlockSpec(memory_space=pltpu.VMEM)
    return pl.pallas_call(
        copy_kernel,
        out_shape=tuple(jax.ShapeDtypeStruct(a.shape, a.dtype) for a in arrays),
        in_specs=[vmem] * 3,
        out_specs=(vmem,) * 3,
        name="copy_out",
    )(*arrays)


def on_device(hidden, qkv_weight, cotangent):
    arrays = call(hidden, qkv_weight.transpose(1, 0, 2), cotangent)
    attention, grad_weight, grad_hidden = copy_out(arrays)
    return attention, grad_hidden, grad_weight.transpose(1, 0, 2)


def solution(mesh):
    in_specs = (P("seq", None), P(None, None, "tp"), P("seq", "tp"))
    out_specs = (P("seq", "tp"), P("seq", "tp"), P("seq", None, "tp"))
    return jax.shard_map(
        on_device, mesh=mesh, in_specs=in_specs, out_specs=out_specs, check_vma=False
    )
```

```python
import math

import jax
import jax.numpy as jnp
from jax import lax
from jax.experimental import pallas as pl
from jax.experimental.pallas import tpu as pltpu
from jax.sharding import PartitionSpec as P

HD = 128
T = 256
NZ, NY, NX = 4, 2, 4
KEYS = NZ * NY * T
CHUNK = 512
SCALE = 1.0 / math.sqrt(HD)
LOG2 = SCALE * math.log2(math.e)
MESH = pl.DeviceIdType.MESH
F32, BF16 = jnp.float32, jnp.bfloat16
NN = (((1,), (0,)), ((), ()))
NT = (((1,), (1,)), ((), ()))


def dot(a, b, dims=NN):
    return lax.dot_general(a, b, dims, preferred_element_type=F32)


def coords():
    s = lax.axis_index("seq")
    return s // (NY * NX), (s // NX) % NY, s % NX, lax.axis_index("tp")


def seq_of(z, y, x):
    return (z * NY + y) * NX + x


def aligned(i, n):
    return pl.ds(pl.multiple_of(i * n, n), n)

Y_QG, Y_KVA, Y_KV1 = 0, 1, 2
X_QGA, X_QGR, X_QG1 = 3, 7, 11
Z_KVA, Z_KVAR, Z_KV1, Z_KV1R = 15, 19, 23, 27
X_HX, C_HX, X_STA, X_ST1 = 31, 35, 39, 43
X_GA, X_GHV, X_GHK, X_GHQ = 47, 51, 55, 67
C_DH, H_DH = 59, 61
Y_OA, Y_KA, Y_V1, Y_K1, Y_W1, Y_WA = 62, 63, 64, 65, 66, 83
X_GB, X_GC, X_GD, N_SEM = 71, 75, 79, 89
Y_KVB, Z_KVBR = 11, 85
RING = (1, 2, 3)
CROSS_FIRST = (0,)


def kernel(
    hidden_ref, w_ref, cot_ref, att_ref, dw_ref, dh_ref,
    h_v, w_v, cot_v, far_qg, far_kv, ht, hx, qg, kv, vkt, pt, ut, s_buf, top_buf, st, sm, sm_all, ma, cs, es, rhs,
    ob, ro, kb, rk, ya_s, ya_r, y1_s, y1_r, ywa_s, ywa_r, yw1_s, yw1_r,
    gx_a, gx_h, dwb_a, dwr_a, dwb_h, dwr_h, dhc, dhr,
    sem_l, sem_s, sem_r, sem_os, sem_or, sem_ks, sem_kr, sem_ws, sem_wr,
):
    z, y, x, t = coords()
    other = 1 - y
    core = t % 2
    mate = t + 1 - 2 * core
    across = (t + 2) % 4
    me = lax.axis_index("seq")
    head_a, head_b = 2 * y, 2 - 2 * y

    def at(zz, yy, xx):
        return (seq_of(zz, yy, xx), t)

    def xs(d):
        return (x + d) % NX

    def zs(d):
        return (z + d) % NZ

    def load(i, src, dst):
        return pltpu.make_async_copy(src, dst, sem_l.at[i])

    def load_w(i, c, h):
        cols = aligned(h, HD)
        return load(i, w_ref.at[c, :, cols], w_v.at[c, :, cols])

    local = [load(0, hidden_ref, h_v), load_w(1, 1, head_b), load_w(2, 2, head_b), load_w(3, 1, head_a), load_w(4, 2, head_a)]
    local += [load_w(5, 0, head_b), load_w(6, 0, head_a), load(7, cot_ref, cot_v)]
    local += [load_w(8 + c, c, 1) for c in range(3)]
    for c in local:
        c.start()

    barrier = pltpu.get_barrier_semaphore()
    peers = [at(z, y, xs(d)) for d in RING] + [at(zs(d), y, x) for d in RING]
    peers += [at(z, other, x), (me, mate), (me, across)]
    for peer in peers:
        pl.semaphore_signal(barrier, inc=1, device_id=peer, device_id_type=MESH)
    pl.semaphore_wait(barrier, len(peers))

    def remote(i, src, dst, peer):
        return pltpu.make_async_remote_copy(
            src_ref=src, dst_ref=dst, send_sem=sem_s.at[i], recv_sem=sem_r.at[i],
            device_id=peer, device_id_type=MESH,
        )

    sent = []

    def send(i, src, dst, peer):
        sent.append(remote(i, src, dst, peer))
        sent[-1].start()

    def got(i, dst):
        remote(i, dst, dst, (me, mate)).wait_recv()

    def qg_slot(yy, xx):
        return qg.at[4 + yy * NX + xx]

    def kv_rows(j, yy, zz):
        return kv.at[j, :, aligned(yy * NZ + zz, T), :]

    def columns(c, h):
        return w_v[c, :, aligned(h, HD)]

    def project_kv(h, dst):
        v = dot(h_v[...], jnp.concatenate([columns(1, h), columns(2, h)], axis=1))
        dst[0] = v[:, :HD].astype(BF16)
        dst[1] = v[:, HD:].astype(BF16)

    partner = at(z, other, x)
    own_a, own_1 = qg_slot(y, x), qg.at[x]
    keys_a, keys_1 = kv_rows(1, y, z), kv_rows(0, y, z)
    for c in local[:3]:
        c.wait()
    project_kv(head_b, far_kv)
    send(Y_KVA, far_kv.at[0], keys_a.at[0], partner)
    send(Y_KVB, far_kv.at[1], keys_a.at[1], partner)
    for c in local[3:5]:
        c.wait()
    project_kv(head_a, keys_a)
    for d in (1, 3):
        send(Z_KVA + d, keys_a, keys_a, at(zs(d), y, x))
    for c in local[5:8]:
        c.wait()
    own_1[1] = cot_v[:, HD : 2 * HD]
    own_a[1] = cot_v[:, aligned(head_a, HD)]
    far_qg[1] = cot_v[:, aligned(head_b, HD)]
    v = dot(h_v[...], jnp.concatenate([columns(0, head_b), columns(0, head_a)], axis=1))
    far_qg[0] = v[:, :HD].astype(BF16)
    own_a[0] = v[:, HD:].astype(BF16)
    send(Y_QG, far_qg, own_a, partner)
    for d in (1, 3):
        send(X_QGA + d, own_a, own_a, at(z, y, xs(d)))

    for part, cross, base in ((0, Y_KVA, Z_KVAR), (1, Y_KVB, Z_KVBR)):
        piece = kv_rows(1, other, z).at[part]
        got(cross, piece)
        for d in (1, 3):
            send(base + d, piece, piece, at(zs(d), y, x))

    def forward_keys(base, yy):
        for part, step in ((0, 1), (1, 3)):
            got(base + step, kv_rows(1, yy, zs(4 - step)))
            piece = kv.at[1, part, aligned(yy * NZ + zs(4 - step), T), :]
            send(base + 2 - 2 * part, piece, piece, at(zs(step), y, x))

    def forward_queries(base, yy):
        for part, step in ((0, 1), (1, 3)):
            got(base + step, qg_slot(yy, xs(4 - step)))
            piece = qg.at[4 + yy * NX + xs(4 - step), part]
            send(base + 2 - 2 * part, piece, piece, at(z, y, xs(step)))

    forward_keys(Z_KVA, y)
    for c in local[8:]:
        c.wait()
    project_kv(1, keys_1)
    own_1[0] = dot(h_v[...], columns(0, 1)).astype(BF16)
    got(Y_QG, qg_slot(other, x))
    for d in (1, 3):
        send(X_QGR + d, qg_slot(other, x), qg_slot(other, x), at(z, y, xs(d)))
    forward_queries(X_QGA, y)
    sm[...] = jnp.zeros_like(sm)
    ma[...] = jnp.zeros_like(ma)

    def hidden_rows(i, _):
        ht[i] = h_v[:, aligned(i, 384)].T.reshape(NX, 96, T)
        return 0

    lax.fori_loop(0, NZ * NY, hidden_rows, 0)
    hx[x] = ht[:, x]

    def transpose_block(j, yy, zz):
        i = yy * NZ + zz
        vkt[0:HD, aligned(i, T)] = kv[j, 1, aligned(i, T), :].T
        vkt[HD : 2 * HD, aligned(i, T)] = kv[j, 0, aligned(i, T), :].T

    def transpose_keys(j, base, base_relay):
        def step(d, _):
            zz = zs(4 - d)
            if base is not None:

                @pl.when(d == 2)
                def _():
                    for part in (0, 1):
                        got(base + 2 - 2 * part, kv.at[j, part, aligned(y * NZ + zz, T), :])
                        got(base_relay + 2 - 2 * part, kv.at[j, part, aligned(other * NZ + zz, T), :])

            transpose_block(j, y, zz)
            transpose_block(j, other, zz)
            return 0

        lax.fori_loop(3, 7, lambda d, _: step(d % 4, _), 0)

    for part, step, base in ((0, 1, Z_KVAR), (1, 3, Z_KVBR)):
        piece = kv_rows(1, other, zs(4 - step)).at[part]
        got(base + step, piece)
        send(Z_KVAR + 2 - 2 * part, piece, piece, at(zs(step), y, x))
    got(Z_KVAR + 3, kv_rows(1, other, zs(1)).at[0])
    got(Z_KVBR + 1, kv_rows(1, other, zs(3)).at[1])
    forward_queries(X_QGR, other)
    transpose_keys(1, Z_KVA, Z_KVAR)

    send(Y_KV1, keys_1, keys_1, partner)
    half = pl.ds(4 * core, 4)
    rows_sent = []
    for d in (2, 1, 3):
        send(Z_KV1 + d, keys_1, keys_1, at(zs(d), y, x))
        rows_sent.append(remote(X_HX + d, ht.at[half, xs(d)], hx.at[x, half], at(z, y, xs(d))))
        rows_sent[-1].start()
    for d in RING:
        send(X_QG1 + d, own_1, own_1, at(z, y, xs(d)))

    chunks = [slice(c * CHUNK, (c + 1) * CHUNK) for c in range(KEYS // CHUNK)]

    def scores(j, q_slot, c, top):
        s = dot(kv[j, 0, c, :], qg[q_slot, 0], NT)
        s_buf[c] = s
        return jnp.maximum(top, jnp.max(s, axis=0, keepdims=True))

    least = jnp.full((1, T), -jnp.inf, F32)

    def unit(j, q_slot, slot, row, following):
        g = qg[q_slot, 1]
        top = top_buf[0:1] * LOG2
        total, out = 0.0, 0.0
        for c in chunks:
            p = jnp.exp2(s_buf[c] * LOG2 - top)
            total = total + jnp.sum(p, axis=0, keepdims=True)
            p = p.astype(BF16)
            pt[slot, c, :] = p
            out = out + dot(vkt[:, c], p)
        g_t = g.astype(F32).T
        delta = jnp.sum(g_t * out[:HD], axis=0, keepdims=True) / total
        grad, top_next = 0.0, least
        for c in chunks:
            if following is not None:
                top_next = scores(*following, c, top_next)
            dp = dot(kv[j, 1, c, :], g, NT)
            d = (pt[slot, c, :].astype(F32) * (dp - delta)).astype(BF16)
            ut[slot, c, :] = d
            grad = grad + dot(vkt[HD:, c], d)
        st[slot, : 2 * HD] = out
        st[slot, 2 * HD :] = grad
        sm[j, 0, pl.ds(row, 1), :] = top + jnp.log2(total)
        sm[j, 1, pl.ds(row, 1), :] = delta
        ma[j, pl.ds(row, 1), :] = top
        top_buf[0:1] = top_next

    def row_a(i):
        yy = (y + i // 4) % 2
        return yy, xs(4 - i % 4), yy * NX + xs(4 - i % 4)

    def relay_shared():
        rows = kv_rows(0, other, z)
        return [remote(Z_KV1R + d, rows, rows, at(zs(d), y, x)) for d in (1, 3)]

    def cross_shared():
        rows = kv_rows(0, y, zs(2))
        return remote(Z_KV1R + 2, rows, rows, partner)

    def unit_a(i, _):
        _, _, r = row_a(i)
        _, _, r_next = row_a(i + 1)

        @pl.when((i == 1) | (i == 5))
        def _():
            for part in (0, 1):
                got(X_QGA + i + 1 - 2 * part, qg.at[4 + r_next, part])

        @pl.when(i == 3)
        def _():
            got(Y_KV1, kv_rows(0, other, z))
            for c in relay_shared():
                c.start()
            got(Z_KV1 + 2, kv_rows(0, y, zs(2)))
            cross_shared().start()

        @pl.when(i == 7)
        def _():
            for d in (1, 3):
                got(Z_KV1 + d, kv_rows(0, y, zs(4 - d)))
            for d in RING:
                got(Z_KV1R + d, kv_rows(0, other, zs(4 - d)))

        last = i // 7
        unit(1, 4 + r, r, r, (1 - last, jnp.where(last == 1, x, 4 + r_next)))
        return 0

    top = least
    for c in chunks:
        top = scores(1, 4 + y * NX + x, c, top)
    top_buf[0:1] = top
    lax.fori_loop(0, 8, unit_a, 0)
    sent.extend(relay_shared() + [cross_shared()])

    def send_stats(j, base):
        for d in RING:
            send(base + d, sm.at[j], sm_all.at[j, x], at(z, y, xs(d)))
        sm_all[j, x] = sm[j]

    def combine(j, base):
        for d in RING:
            got(base + d, sm_all.at[j, xs(4 - d)])
        lse = sm_all[j, :, 0]
        top = jnp.max(lse, axis=0)
        lse_all = top + jnp.log2(jnp.sum(jnp.exp2(lse - top), axis=0))
        delta = jnp.sum(jnp.exp2(lse - lse_all) * sm_all[j, :, 1], axis=0)
        cs[j] = jnp.exp2(ma[j] - lse_all)
        es[j] = delta - sm[j, 1]

    send_stats(1, X_STA)
    for d in RING:
        part = hx.at[xs(4 - d), half]
        got(X_HX + d, part)
        send(C_HX + d, part, part, (me, mate))
    transpose_keys(0, None, None)
    got(X_QG1 + 1, qg.at[xs(3)])
    unit(0, x, 8, x, (0, xs(3)))
    combine(1, X_STA)

    def prepare(j, row, slot, q_slot, r, b):
        c, e = cs[j, pl.ds(row, 1), :], es[j, pl.ds(row, 1), :]
        o = st[slot, 0:HD] * c
        dq = (st[slot, 2 * HD :] - e * st[slot, HD : 2 * HD]) * (c * SCALE)
        ob[b, 0] = o.T.astype(BF16)
        ob[b, 1] = dq.T.astype(BF16)
        cols = jnp.concatenate([c, e, jnp.zeros((6, T), F32)], axis=0).T
        c, e = cols[:, 0:1], cols[:, 1:2]
        cq = c * qg[q_slot, 0].astype(F32)
        rhs[r, :, 0:HD] = (c * qg[q_slot, 1].astype(F32)).astype(BF16)
        rhs[r, :, HD : 2 * HD] = (e * cq).astype(BF16)
        rhs[r, :, 2 * HD :] = cq.astype(BF16)

    def copy_o(kind, d, b):
        return pltpu.make_async_remote_copy(
            src_ref=ob.at[b], dst_ref=ro.at[kind, x], send_sem=sem_os.at[kind, d], recv_sem=sem_or.at[kind, d],
            device_id=at(z, y, xs(4 - d)), device_id_type=MESH,
        )

    def got_o(kind):
        def step(d):
            dst = ro.at[kind, xs(d)]
            pltpu.make_async_remote_copy(
                src_ref=dst, dst_ref=dst, send_sem=sem_os.at[kind, d], recv_sem=sem_or.at[kind, d],
                device_id=partner, device_id_type=MESH,
            ).wait_recv()

        loop(1, 4, step)

    def send_a(i):
        return copy_o(i // 4, i % 4, row_a(i)[2])

    def loop(first, last, step):
        def body(i, _):
            step(i)
            return 0

        lax.fori_loop(first, last, body, 0)

    def prepare_a(k):
        i = 7 - k
        _, _, r = row_a(i)
        prepare(1, r, r, 4 + r, r, r)

        @pl.when(i % 4 != 0)
        def _():
            send_a(i).start()

    loop(0, 8, prepare_a)
    ro[0, x] = ob[y * NX + x]
    ro[1, x] = ob[other * NX + x]

    def k_block(row, zz):
        return ((y + row) % 2) * NZ + zz

    def k_part(kind):
        return pl.ds(0, 2) if kind < 2 else pl.ds(1, 1) if kind < 4 else pl.ds(0, 1)

    def k_slots(kind):
        return (2 if kind < 2 else 0) + kind % 2

    def copy_k(kind, d):
        src = kb.at[k_block(kind % 2, zs(d)), k_part(kind)]
        return pltpu.make_async_remote_copy(
            src_ref=src, dst_ref=rk.at[k_slots(kind), z, k_part(kind)], send_sem=sem_ks.at[kind, d],
            recv_sem=sem_kr.at[kind, d], device_id=at(zs(d), y, x), device_id_type=MESH,
        )

    def got_k(kind):
        def step(d):
            dst = rk.at[k_slots(kind), zs(4 - d), k_part(kind)]
            pltpu.make_async_remote_copy(
                src_ref=dst, dst_ref=dst, send_sem=sem_ks.at[kind, d],
                recv_sem=sem_kr.at[kind, d], device_id=partner, device_id_type=MESH,
            ).wait_recv()

        loop(1, 4, step)

    def key_blocks(step, kind):
        for row in (1, 0):

            def one(k, row=row):
                zz = 2 * ((z // 2 + 1 + k) % 2)
                b = k_block(row, zz)
                step(b)
                for i in (0, 1):
                    d = (zz + i + NZ - z) % NZ

                    @pl.when(d != 0)
                    def _():
                        copy_k(kind + row, d).start()

            loop(0, 2, one)
            b, part = k_block(row, z), k_part(kind)
            rk[k_slots(kind + row), z, part] = kb[b, part]

    def two_rows(i):
        return pl.ds(pl.multiple_of(i * T, 2 * T), 2 * T)

    def put(b, part, v):
        kb[b, part] = v[:T].astype(BF16)
        kb[b + 1, part] = v[T:].astype(BF16)

    def block_a(i):
        dv = dk = 0.0
        for r in range(8):
            dv = dv + dot(pt[r, two_rows(i), :], rhs[r, :, : 2 * HD])
            dk = dk + dot(ut[r, two_rows(i), :], rhs[r, :, 2 * HD :])
        put(i, 0, (dk - dv[:, HD:]) * SCALE)
        put(i, 1, dv[:, :HD])

    shared_slots = (8, 0, 1, 2)

    def block_v(i):
        dv = 0.0
        for r, slot in enumerate(shared_slots):
            dv = dv + dot(pt[slot, two_rows(i), :], rhs[r, :, : 2 * HD])
        st[i, : 2 * HD, :HD] = dv[:T, HD:]
        st[i + 1, : 2 * HD, :HD] = dv[T:, HD:]
        put(i, 1, dv[:, :HD])

    def block_k(i):
        dk = 0.0
        for r, slot in enumerate(shared_slots):
            dk = dk + dot(ut[slot, two_rows(i), :], rhs[r, :, 2 * HD :])
        put(i, 0, (dk - jnp.concatenate([st[i, : 2 * HD, :HD], st[i + 1, : 2 * HD, :HD]], axis=0)) * SCALE)

    key_blocks(block_a, 0)

    def total(ref, kind, part):
        v = ref[kind, 0, part].astype(F32)
        for i in range(1, 4):
            v = v + ref[kind, i, part].astype(F32)
        return v

    mine, theirs = aligned(y, HD), aligned(other, HD)
    q_part, kv_part = pl.ds(0, 1), pl.ds(1, 2)

    def piece_a(d, part, cols):
        return gx_a.at[xs(d), part, :, cols]

    def gather_a(base, part, cols):
        piece = piece_a(0, part, cols)
        return [remote(base + d, piece, piece, at(z, y, xs(d))) for d in (1, 3)]

    def pass_on(base, part, cols, step):
        piece = piece_a(4 - step, part, cols)
        return remote(base + 2, piece, piece, at(z, y, xs(step)))

    def forward_a(base, part, cols, step):
        got(base + step, piece_a(4 - step, part, cols))
        pass_on(base, part, cols, step).start()

    pieces = {X_GA: (q_part, mine, 1), X_GB: (q_part, theirs, 3), X_GC: (kv_part, mine, 1), X_GD: (kv_part, theirs, 3)}

    def got_a(base):
        part, cols, step = pieces[base]
        got(base + 4 - step, piece_a(step, part, cols))
        got(base + 2, piece_a(2, part, cols))

    def far_o():
        return remote(Y_OA, ya_s.at[pl.ds(0, 2)], ya_r.at[pl.ds(0, 2)], partner)

    def far_k():
        return remote(Y_KA, ya_s.at[pl.ds(2, 2)], ya_r.at[pl.ds(2, 2)], partner)

    def start_all(copies):
        for c in copies:
            c.start()

    def unit_shared(d):
        got(X_QG1 + d + 1, qg.at[xs(3 - d)])
        unit(0, xs(4 - d), d - 1, xs(4 - d), (0, xs(3 - d)))

        @pl.when(d == 1)
        def _():
            got_o(1)
            for part in (0, 1):
                ya_s[part] = total(ro, 1, part).astype(BF16)
            far_o().start()
            got_o(0)
            att_ref[:, aligned(head_a, HD)] = total(ro, 0, 0).astype(BF16)
            gx_a[x, 0, :, mine] = total(ro, 0, 1).astype(BF16)
            start_all(gather_a(X_GA, q_part, mine))

        @pl.when(d == 2)
        def _():
            got_k(1)
            for part in (0, 1):
                ya_s[2 + part] = total(rk, 3, part).astype(BF16)
            far_k().start()
            got(Y_OA, ya_r.at[pl.ds(0, 2)])
            att_ref[:, aligned(head_b, HD)] = ya_r[0]
            gx_a[x, 0, :, theirs] = ya_r[1]
            start_all(gather_a(X_GB, q_part, theirs))
            got_k(0)
            for part in (0, 1):
                gx_a[x, 1 + part, :, mine] = total(rk, 2, part).astype(BF16)
            start_all(gather_a(X_GC, kv_part, mine))
            forward_a(X_GA, q_part, mine, 1)

    loop(1, 3, unit_shared)
    unit(0, xs(1), 2, xs(1), None)
    send_stats(0, X_ST1)
    got(Y_KA, ya_r.at[pl.ds(2, 2)])
    for c in (1, 2):
        gx_a[x, c, :, theirs] = ya_r[1 + c]
    start_all(gather_a(X_GD, kv_part, theirs))
    sent.extend([far_o(), far_k()])
    forward_a(X_GB, q_part, theirs, 3)
    for base, (part, cols, step) in pieces.items():
        sent.extend(gather_a(base, part, cols))
        sent.append(pass_on(base, part, cols, step))

    def copy_w(c, d):
        if c in CROSS_FIRST:
            src, dst = dwb_a.at[zs(d), c, y], dwr_a.at[z, c, y]
        elif c < 3:
            src, dst = dwb_a.at[zs(d), c], dwr_a.at[z, c]
        else:
            src, dst = dwb_h.at[zs(d), c - 3], dwr_h.at[z, c - 3]
        return pltpu.make_async_remote_copy(
            src_ref=src, dst_ref=dst, send_sem=sem_ws.at[c, d],
            recv_sem=sem_wr.at[c, d], device_id=at(zs(d), y, x), device_id_type=MESH,
        )

    def got_w(c):
        def step(d):
            dst = (dwr_h if c >= 3 else dwr_a).at[zs(4 - d), c % 3]
            dst = dst.at[y] if c in CROSS_FIRST else dst
            pltpu.make_async_remote_copy(
                src_ref=dst, dst_ref=dst, send_sem=sem_ws.at[c, d], recv_sem=sem_wr.at[c, d],
                device_id=partner, device_id_type=MESH,
            ).wait_recv()

        loop(1, 4, step)

    def weight_rows(gx, dwb, c):
        def step(i):
            v = 0.0
            for xx in range(NX):
                v = v + dot(hx[xx, pl.ds(i * 4, 4)].reshape(4 * 96, T), gx[xx, c])
            dwb[pl.ds(i * 2, 2), c] = v.astype(BF16).reshape(2, 2, 96, v.shape[1])

        loop(0, 2, step)

    def weight_a(c):
        weight_rows(gx_a, dwb_a, c)
        if c in CROSS_FIRST:
            send(Y_WA + c, dwb_a.at[:, c, other], ywa_r.at[c], partner)
        else:
            loop(1, 4, lambda d: copy_w(c, d).start())
            dwr_a[z, c] = dwb_a[z, c]

    def weight_a_ring(c):
        got(Y_WA + c, ywa_r.at[c])
        dwb_a[:, c, y] = (dwb_a[:, c, y].astype(F32) + ywa_r[c].astype(F32)).astype(BF16)
        loop(1, 4, lambda d: copy_w(c, d).start())
        dwr_a[z, c, y] = dwb_a[z, c, y]

    def weight_shared(c):
        weight_rows(gx_h, dwb_h, c)
        loop(1, 4, lambda d: copy_w(3 + c, d).start())
        dwr_h[z, c] = dwb_h[z, c]

    for c in rows_sent:
        c.wait_send()

    def part_of(to):
        return ht.at[pl.ds(2 * to, 2)]

    def hidden_sum(to, term):
        pieces = []
        for i in range(3):
            rows = pl.ds(pl.multiple_of(to * 768 + i * 256, 256), 256)
            pieces.append(term(0, rows) + term(1, rows) + term(2, rows))
        return jnp.concatenate(pieces, axis=0)

    def term_a(c, rows):
        w = jnp.concatenate([w_v[c, rows, :HD], w_v[c, rows, 2 * HD :]], axis=1)
        return dot(gx_a[x, c], w, NT)

    def term_shared(c, rows):
        return dot(gx_h[x, c], w_v[c, rows, HD : 2 * HD], NT)

    def hidden_first(to):
        part_of(to)[...] = hidden_sum(to, term_a).astype(BF16).reshape(2, NX, 96, T)

    def hidden_part(to):
        v = part_of(to)[...].astype(F32).reshape(3 * T, T) + hidden_sum(to, term_shared)
        part_of(to)[...] = v.astype(BF16).reshape(2, NX, 96, T)

    loop(0, 4, hidden_first)
    combine(0, X_ST1)

    def send_shared(d):
        return copy_o(2, d, xs(4 - d))

    def prepare_shared(d):
        slot = (d + 8) % 9
        prepare(0, xs(4 - d), slot, xs(4 - d), d, xs(4 - d))

        @pl.when(d != 0)
        def _():
            send_shared(d).start()

    for c in range(2):
        loop(1, 4, lambda d, c=c: send_a(4 * c + d).wait_send())
    loop(0, 4, prepare_shared)
    ro[2, x] = ob[x]

    for kind in (0, 1):
        loop(1, 4, lambda d, kind=kind: copy_k(kind, d).wait_send())
    key_blocks(block_v, 2)
    forward_a(X_GC, kv_part, mine, 1)
    forward_a(X_GD, kv_part, theirs, 3)
    for d in RING:
        got(C_HX + d, hx.at[xs(4 - d), pl.ds(4 - 4 * core, 4)])
    got_a(X_GA)
    got_a(X_GB)
    weight_a(0)
    key_blocks(block_k, 4)


    got_o(2)
    att_ref[:, HD : 2 * HD] = total(ro, 2, 0).astype(BF16)
    gx_h[x, 0] = total(ro, 2, 1).astype(BF16)

    def gather_shared(base, c):
        for d in RING:
            send(base + d, gx_h.at[x, c], gx_h.at[x, c], at(z, y, xs(d)))

    def got_shared(base, c):
        for d in RING:
            got(base + d, gx_h.at[xs(4 - d), c])

    gather_shared(X_GHQ, 0)
    got_k(3)
    y1_s[1] = total(rk, 1, 1).astype(BF16)
    send(Y_V1, y1_s.at[1], y1_r.at[1], partner)
    weight_a_ring(0)
    got_a(X_GC)
    got_a(X_GD)
    weight_a(2)
    got_k(2)
    got(Y_V1, y1_r.at[1])
    gx_h[x, 2] = (total(rk, 0, 1) + y1_r[1].astype(F32)).astype(BF16)
    gather_shared(X_GHV, 2)
    got_k(5)
    y1_s[0] = total(rk, 1, 0).astype(BF16)
    send(Y_K1, y1_s.at[0], y1_r.at[0], partner)
    weight_a(1)
    got_k(4)
    got(Y_K1, y1_r.at[0])
    gx_h[x, 1] = (total(rk, 0, 0) + y1_r[0].astype(F32)).astype(BF16)
    gather_shared(X_GHK, 1)

    def copy_mate(i):
        return remote(C_DH + i, part_of(2 * i + 1 - core), dhc.at[i], (me, mate))

    def hidden_pair(i):
        hidden_part(2 * i + 1 - core)
        copy_mate(i).start()
        hidden_part(2 * i + core)

    hi = t // 2
    hidden_pair(1 - hi)
    got(C_DH + 1 - hi, dhc.at[1 - hi])
    far = part_of(across)
    far[...] = (far[...].astype(F32) + dhc[1 - hi].astype(F32)).astype(BF16)
    send(H_DH, far, dhr, (me, across))
    got_shared(X_GHQ, 0)
    weight_shared(0)
    got_shared(X_GHV, 2)
    weight_shared(2)
    got_shared(X_GHK, 1)
    weight_shared(1)
    hidden_pair(hi)
    sent.extend([copy_mate(0), copy_mate(1)])

    def total_w(ref, c, row):
        v = ref[0, c, row].astype(F32)
        for i in range(1, NZ):
            v = v + ref[i, c, row].astype(F32)
        return v

    ring_first = [c for c in range(3) if c not in CROSS_FIRST]
    for c in ring_first:
        got_w(c)
        ywa_s[c] = total_w(dwr_a, c, other).astype(BF16)
        send(Y_WA + c, ywa_s.at[c], ywa_r.at[c, 0], partner)
    for c in range(3):
        got_w(3 + c)
        yw1_s[c] = total_w(dwr_h, c, other).astype(BF16)
    send(Y_W1, yw1_s, yw1_r, partner)
    for c in range(3):
        if c in CROSS_FIRST:
            got_w(c)
        v = total_w(dwr_a, c, y)
        if c in ring_first:
            got(Y_WA + c, ywa_r.at[c, 0])
            v = v + ywa_r[c, 0].astype(F32)
        dw_ref[c, :, :HD] = v[:, :HD]
        dw_ref[c, :, 2 * HD :] = v[:, HD:]
    got(Y_W1, yw1_r)
    for c in range(3):
        dw_ref[c, :, HD : 2 * HD] = total_w(dwr_h, c, y) + yw1_r[c].astype(F32)
    got(C_DH + hi, dhc.at[hi])
    got(H_DH, dhr)
    v = (part_of(t)[...].astype(F32) + dhc[hi].astype(F32) + dhr[...].astype(F32)).astype(BF16).reshape(3 * T, T)
    for i in range(3):
        dh_ref[:, i * T : (i + 1) * T] = v[i * T : (i + 1) * T]

    for c in sent:
        c.wait_send()
    loop(1, 4, lambda d: send_shared(d).wait_send())
    for kind in range(6):
        if kind > 1:
            loop(1, 4, lambda d, kind=kind: copy_k(kind, d).wait_send())
        loop(1, 4, lambda d, c=kind: copy_w(c, d).wait_send())


def call(hidden, weight, cotangent):
    block = (2, T, HD)
    scratch = [
        ((T, 3072), BF16),
        ((3, 3072, 384), BF16),
        ((T, 3 * HD), BF16),
        (block, BF16),
        (block, BF16),
        ((8, NX, 96, T), BF16),
        ((NX, 8, 96, T), BF16),
        ((12,) + block, BF16),
        ((2, 2, KEYS, HD), BF16),
        ((2 * HD, KEYS), BF16),
        ((9, KEYS, T), BF16),
        ((9, KEYS, T), BF16),
        ((KEYS, T), F32),
        ((8, T), F32),
        ((9, 3 * HD, T), F32),
        ((2, 2, 8, T), F32),
        ((2, NX, 2, 8, T), F32),
        ((2, 8, T), F32),
        ((2, 8, T), F32),
        ((2, 8, T), F32),
        ((8, T, 3 * HD), BF16),
        ((8,) + block, BF16),
        ((3, NX) + block, BF16),
        ((8,) + block, BF16),
        ((4, NZ) + block, BF16),
        ((4, T, HD), BF16),
        ((4, T, HD), BF16),
        (block, BF16),
        (block, BF16),
        ((3, 96, 2 * HD), BF16),
        ((3, NZ, 96, 2 * HD), BF16),
        ((3, 96, HD), BF16),
        ((3, 96, HD), BF16),
        ((NX, 3, T, 2 * HD), BF16),
        ((NX, 3, T, HD), BF16),
        ((NZ, 3, 2, 96, 2 * HD), BF16),
        ((NZ, 3, 2, 96, 2 * HD), BF16),
        ((NZ, 3, 2, 96, HD), BF16),
        ((NZ, 3, 2, 96, HD), BF16),
        ((2, 2, NX, 96, T), BF16),
        ((2, NX, 96, T), BF16),
    ]
    sems = [(11,), (N_SEM,), (N_SEM,), (3, 4), (3, 4), (6, 4), (6, 4), (6, 4), (6, 4)]
    vmem = pl.BlockSpec(memory_space=pltpu.VMEM)
    hbm = pl.BlockSpec(memory_space=pl.ANY)
    return pl.pallas_call(
        kernel,
        out_shape=(
            jax.ShapeDtypeStruct((T, 3 * HD), BF16),
            jax.ShapeDtypeStruct((3, 96, 384), F32),
            jax.ShapeDtypeStruct((T, 768), BF16),
        ),
        in_specs=[hbm] * 3,
        out_specs=(vmem,) * 3,
        scratch_shapes=[pltpu.VMEM(*s) for s in scratch] + [pltpu.SemaphoreType.DMA(s) for s in sems],
        compiler_params=pltpu.CompilerParams(
            collective_id=0, has_side_effects=True, vmem_limit_bytes=63 * 2**20
        ),
        cost_estimate=pl.CostEstimate(flops=18 * 10**9, bytes_accessed=10**7, transcendentals=6 * 10**6),
        name="attention_with_gradients",
    )(hidden, weight, cotangent)


def copy_kernel(*refs):
    for src, dst in zip(refs[:3], refs[3:]):
        dst[...] = src[...]


def copy_out(arrays):
    vmem = pl.BlockSpec(memory_space=pltpu.VMEM)
    return pl.pallas_call(
        copy_kernel,
        out_shape=tuple(jax.ShapeDtypeStruct(a.shape, a.dtype) for a in arrays),
        in_specs=[vmem] * 3,
        out_specs=(vmem,) * 3,
        name="copy_out",
    )(*arrays)


def on_device(hidden, qkv_weight, cotangent):
    arrays = call(hidden, qkv_weight.transpose(1, 0, 2), cotangent)
    attention, grad_weight, grad_hidden = copy_out(arrays)
    return attention, grad_hidden, grad_weight.transpose(1, 0, 2)


def solution(mesh):
    in_specs = (P("seq", None), P(None, None, "tp"), P("seq", "tp"))
    out_specs = (P("seq", "tp"), P("seq", "tp"), P("seq", None, "tp"))
    return jax.shard_map(
        on_device, mesh=mesh, in_specs=in_specs, out_specs=out_specs, check_vma=False
    )
```
